128 devices in a mesh: ctx: 16 (over y, z_hi, core), grp: 8 (over z_lo, x).
Axes of the slice: x: 4, y: 4, z: 4 (z_hi: 2, z_lo: 2; z = z_hi * 2 + z_lo), core: 2. Of those that a mesh axis runs over, the one named last changes fastest.
Arguments:
- prompt_lens: int32 [4], replicated, may hold values from 1 to 6144, 8192 in all
- pre_q: bfloat16 [8192, 8192], P('ctx', 'grp'), may hold values from -8 to 8
- pre_kv: bfloat16 [8192, 2048], P('ctx', 'grp'), may hold values from -8 to 8
- owners: int32 [256], replicated, may hold values from 0 to 15, as said below
- resident: bfloat16 [4096, 32, 2048], P('ctx', None, 'grp'), may hold values from -8 to 8
- page_table: int32 [512, 32], P('ctx'), may hold values from 0 to 4127, as said below
- cache_len: int32 [512], P('ctx'), may hold values from 1 to 1024, as said below
- dec_q: bfloat16 [512, 8192], P('ctx', 'grp'), may hold values from -8 to 8
- dec_new: bfloat16 [512, 2048], P('ctx', 'grp'), may hold values from -8 to 8
- out_weight: bfloat16 [8192, 8192], P('grp', 'ctx'), may hold values from -0.1875 to 0.1875
Outputs:
- attended: bfloat16 [8192, 8192], P('ctx', 'grp')
- decoded: bfloat16 [512, 8192], P('grp', 'ctx')
The draws below stay inside these ranges and needn't reach their ends.
Inputs may be any that keep to these rules, and one draw needn't show every extreme that they name: `owners`: of the 16 pages in each aligned block (the pages of one index of ctx), at most 2 have one owner; one owner receives 2 pages from every block. `page_table`: an entry of row r, with holder h = r // 32, is a resident page of h (h * 256 to h * 256 + 255) or 4096 + j with j below the number of prompt pages that h owns. Every row has cache_len[r] <= 1024; some row reaches 1024.
All inputs are finite; a program needn't handle non-finite values.
Results may differ from the reference program's by a relative error of at most 0.019.
Values may be sent and summed in bfloat16 or wider, within the bound.
No kernel may reach another device: no remote copies, remote signals or barrier semaphores. Data moves between devices by JAX's collectives and lax.ppermute only.
A program may use at most 256 MiB of HBM per device.

```python
import math
import jax
import jax.numpy as jnp
import numpy as np
from jax import lax

D = 8192
QH = 64
KVH = 8
HD = 128
NPROMPT = 4
PAGE = 32
CAP = 2
ROWS_DEV = 32
MAXP = 32
RES_PAGES = 256
TOKENS = 8192
ROWS = 512
OWNERS = 16
PPD = 16
NPAGE = 256
RESIDENT = 4096


def shared_direction(key):
    return jnp.where(jax.random.bernoulli(key, 0.5, (HD,)), 1.0, -1.0).astype(jnp.float32)


def key_value_rows(key, direction, leading, strength_top):
    key_one, key_two, key_three = jax.random.split(key, 3)
    noise = jax.random.truncated_normal(key_one, -4.0, 4.0, leading + (KVH, HD), jnp.float32)
    strength = jax.random.uniform(key_three, leading + (KVH, 1), jnp.float32, 0.0, strength_top)
    key_part = noise + strength * direction
    value_part = jax.random.truncated_normal(key_two, -4.0, 4.0, leading + (KVH, HD), jnp.float32)
    return jnp.stack([key_part, value_part], axis=-2)


def query_rows(key, direction, leading, strength_top, noise_scale):
    key_one, key_two = jax.random.split(key, 2)
    noise = noise_scale * jax.random.truncated_normal(key_one, -3.0, 3.0, leading + (QH, HD), jnp.float32)
    strength = jax.random.uniform(key_two, leading + (QH, 1), jnp.float32, 0.0, strength_top)
    return noise + strength * direction


def owner_list(key):
    key = jax.random.fold_in(key, 101)
    hot_key, slot_key, order_key = jax.random.split(key, 3)
    hottest = jax.random.randint(hot_key, (), 0, OWNERS)
    others = PPD - CAP

    def one_source(slot_seed, order_seed):
        chosen = jax.random.permutation(slot_seed, (OWNERS - 1) * CAP)[:others]
        other_owner = chosen // CAP
        other_owner = other_owner + (other_owner >= hottest).astype(jnp.int32)
        listed = jnp.concatenate([jnp.full((CAP,), hottest, jnp.int32), other_owner.astype(jnp.int32)])
        return jax.random.permutation(order_seed, listed)
    result = jax.vmap(one_source)(jax.random.split(slot_key, OWNERS), jax.random.split(order_key, OWNERS))
    return (result.reshape(NPAGE).astype(jnp.int32), hottest.astype(jnp.int32))


def draw_pre_q(key, part):
    direction = shared_direction(key)
    key = jax.random.fold_in(key, 1)
    values = query_rows(key, direction, (TOKENS,), 0.0, 2.0)
    return values.reshape(TOKENS, QH * HD).astype(jnp.bfloat16)


def draw_pre_kv(key, part):
    direction = shared_direction(key)
    key = jax.random.fold_in(key, 2)
    values = key_value_rows(key, direction, (TOKENS,), 0.0)
    return values.reshape(TOKENS, 2 * KVH * HD).astype(jnp.bfloat16)


def draw_resident(key, part):
    direction = shared_direction(key)
    key = jax.random.fold_in(key, 3)
    values = key_value_rows(key, direction, (RESIDENT, PAGE), 0.0)
    return values.reshape(RESIDENT, PAGE, 2 * KVH * HD).astype(jnp.bfloat16)


def draw_dec_q(key, part):
    direction = shared_direction(key)
    key = jax.random.fold_in(key, 4)
    values = query_rows(key, direction, (ROWS,), 0.0, 2.0)
    return values.reshape(ROWS, QH * HD).astype(jnp.bfloat16)


def draw_dec_new(key, part):
    direction = shared_direction(key)
    key = jax.random.fold_in(key, 5)
    values = key_value_rows(key, direction, (ROWS,), 0.0)
    return values.reshape(ROWS, 2 * KVH * HD).astype(jnp.bfloat16)


def draw_owners(key, part):
    return owner_list(key)[0]


def draw_page_table(key, part):
    owner_ids, hottest = owner_list(key)
    key = jax.random.fold_in(key, 7)
    resident_key, rank_key, pick_key, row_key = jax.random.split(key, 4)
    holder = jnp.arange(ROWS, dtype=jnp.int32) // ROWS_DEV
    resident_pick = jax.random.randint(resident_key, (ROWS, MAXP), 0, RES_PAGES) + holder[:, None] * RES_PAGES
    counts = jnp.sum((owner_ids[None, :] == jnp.arange(OWNERS, dtype=jnp.int32)[:, None]).astype(jnp.int32), axis=1)
    row_counts = counts[holder]
    rank_pick = jax.random.randint(rank_key, (ROWS, MAXP), 0, jnp.maximum(row_counts, 1)[:, None])
    picked = (jax.random.randint(pick_key, (ROWS, MAXP), 0, 2) == 1) & (row_counts[:, None] > 0)
    table = jnp.where(picked, RESIDENT + rank_pick, resident_pick).astype(jnp.int32)
    hot_row = hottest * ROWS_DEV + jax.random.randint(row_key, (), 0, ROWS_DEV)
    return table.at[hot_row, 0].set(RESIDENT + OWNERS * CAP - 1).astype(jnp.int32)


def draw_cache_len(key, part):
    key = jax.random.fold_in(key, 9)
    length_key, longest_key = jax.random.split(key, 2)
    lengths = jax.random.randint(length_key, (ROWS,), 1, MAXP * PAGE + 1)
    longest_row = jax.random.randint(longest_key, (), 0, ROWS)
    return lengths.at[longest_row].set(MAXP * PAGE).astype(jnp.int32)


def levels(stream_key, extent, cuts, least, largest):
    loudness, own = 1.0, jax.random.fold_in(stream_key, 6)
    for position, shards_of in cuts:
        heights = jnp.exp(jax.random.uniform(jax.random.fold_in(own, position), (shards_of,), jnp.float32, least / len(cuts), largest / len(cuts)))
        loudness = loudness * jnp.repeat(heights, extent[position] // shards_of).reshape([-1 if axis == position else 1 for axis in range(len(extent))])
    return loudness


def split_up(number_of, total, most, skew):
    weights = [(1 << 20) // math.isqrt(rank ** skew) + 1 for rank in range(2, number_of + 1)]
    surplus, given = total - most - (number_of - 1), [1] * (number_of - 1)
    while surplus > 0:
        free = [i for i in range(number_of - 1) if given[i] < most]
        mass, left = sum([weights[i] for i in free]), surplus
        for i in free:
            extra = min(most - given[i], max(1, left * weights[i] // mass), surplus)
            given[i] = given[i] + extra
            surplus = surplus - extra
    return np.array([most] + given)


def ragged_sizes(key, amount, total, most, lean):
    if amount == 2:
        one = jax.random.randint(key, (), max(1, total - most), min(most, total - 1) + 1)
        return jnp.stack([one, total - one])
    sizes = jnp.asarray(split_up(amount, total, most, lean), jnp.int32)
    couples = (amount - 1) // 2
    donor, taker = sizes[1:1 + 2 * couples:2], sizes[2:2 + 2 * couples:2]
    margin = jnp.minimum(donor - 1, most - taker)
    passed = jax.random.randint(jax.random.fold_in(key, 1), (couples,), 0, 1 << 20) % (margin + 1)
    sizes = sizes.at[1:1 + 2 * couples:2].set(donor - passed).at[2:2 + 2 * couples:2].set(taker + passed)
    return sizes[jax.random.permutation(jax.random.fold_in(key, 2), amount)]


def centred(rng, dims, spread, most, cuts=(), kind=jnp.bfloat16):
    entries = jax.random.normal(rng, dims, jnp.float32) * spread
    if len(cuts) > 0:
        entries = levels(rng, dims, cuts, -0.22, 0.18) * entries
    return jnp.clip(entries, min=-most, max=most).astype(kind)


def setup_inputs(seed: int = 0) -> dict:
    key_of = jax.random.split(jax.random.key(seed), 11)
    return {
        "prompt_lens": ragged_sizes(key_of[0], NPROMPT, TOKENS, TOKENS * 3 // 4, 2).astype(jnp.int32),
        "pre_q": draw_pre_q(jax.random.fold_in(key_of[10], 71), 0),
        "pre_kv": draw_pre_kv(jax.random.fold_in(key_of[10], 71), 0),
        "owners": draw_owners(jax.random.fold_in(key_of[10], 71), 0),
        "resident": draw_resident(jax.random.fold_in(key_of[10], 71), 0),
        "page_table": draw_page_table(jax.random.fold_in(key_of[10], 71), 0),
        "cache_len": draw_cache_len(jax.random.fold_in(key_of[10], 71), 0),
        "dec_q": draw_dec_q(jax.random.fold_in(key_of[10], 71), 0),
        "dec_new": draw_dec_new(jax.random.fold_in(key_of[10], 71), 0),
        "out_weight": centred(key_of[9], (QH * HD, D), (QH * HD // 8) ** -0.5, 0.1875, ((0, 8), (1, 16))),
    }


NEG = -1e30


def prompt_segment(positions, prompt_ends):
    return jnp.sum((positions[:, None] >= prompt_ends[None, :]).astype(jnp.int32), axis=1)


def reference(prompt_lens, pre_q, pre_kv, owners, resident, page_table, cache_len, dec_q, dec_new, out_weight):
    group_size = QH // KVH
    scaling = HD ** -0.5
    prompt_ends = jnp.cumsum(prompt_lens)
    positions = jnp.arange(TOKENS, dtype=jnp.int32)
    segment = prompt_segment(positions, prompt_ends)
    key_value = pre_kv.reshape(TOKENS, KVH, 2, HD)
    key_rows = key_value[:, :, 0, :].astype(jnp.float32).transpose(1, 0, 2)
    value_rows = key_value[:, :, 1, :].astype(jnp.float32).transpose(1, 0, 2)
    query_block = math.gcd(TOKENS, 512)

    def prefill_block(block_index):
        first_row = (block_index * query_block).astype(jnp.int32)
        queries = lax.dynamic_slice_in_dim(pre_q, first_row, query_block, 0)
        queries = queries.reshape(query_block, KVH, group_size, HD).astype(jnp.float32).transpose(1, 0, 2, 3)
        query_pos = first_row + jnp.arange(query_block, dtype=jnp.int32)
        query_seg = lax.dynamic_slice_in_dim(segment, first_row, query_block, 0)
        allowed = (positions[None, :] <= query_pos[:, None]) & (segment[None, :] == query_seg[:, None])

        def one_head(operands):
            head_q, head_k, head_v = operands
            scores = jnp.einsum('tqd,kd->qtk', head_q, head_k) * scaling
            scores = jnp.where(allowed[None], scores, NEG)
            row_max = jnp.max(scores, axis=-1, keepdims=True)
            weights = jnp.where(allowed[None], jnp.exp(scores - row_max), 0.0)
            denominator = jnp.sum(weights, axis=-1)
            rounded = lax.optimization_barrier(weights.astype(jnp.bfloat16)).astype(jnp.float32)
            weighted = jnp.einsum('qtk,kd->qtd', rounded, head_v)
            return (weighted / denominator[..., None]).astype(jnp.bfloat16)

        result = lax.map(one_head, (queries, key_rows, value_rows))
        return result.transpose(2, 0, 1, 3).reshape(query_block, QH * HD)

    blocks_out = lax.map(prefill_block, jnp.arange(TOKENS // query_block, dtype=jnp.int32))
    attended = blocks_out.reshape(TOKENS, QH * HD)

    pages_all = jnp.concatenate([resident, pre_kv.reshape(NPAGE, PAGE, 2 * KVH * HD)], axis=0)
    span = MAXP * PAGE
    page_ids = jnp.arange(NPAGE, dtype=jnp.int32)

    def decode_block(block_index):
        first_row = (block_index * ROWS_DEV).astype(jnp.int32)
        table = lax.dynamic_slice_in_dim(page_table, first_row, ROWS_DEV, 0)
        owned = (owners == block_index).astype(jnp.int32)
        rank = jnp.cumsum(owned) - owned
        wanted = table - RESIDENT
        match = (owned[None, None, :] == 1) & (rank[None, None, :] == wanted[..., None])
        handed = jnp.sum(jnp.where(match, page_ids[None, None, :], 0), axis=-1).astype(jnp.int32)
        table = jnp.where(table < RESIDENT, table, RESIDENT + handed).astype(jnp.int32)
        lengths = lax.dynamic_slice_in_dim(cache_len, first_row, ROWS_DEV, 0)
        cache_rows = pages_all[table].reshape(ROWS_DEV, span, KVH, 2, HD).astype(jnp.float32)
        queries = lax.dynamic_slice_in_dim(dec_q, first_row, ROWS_DEV, 0)
        queries = queries.reshape(ROWS_DEV, KVH, group_size, HD).astype(jnp.float32)
        fresh_kv = lax.dynamic_slice_in_dim(dec_new, first_row, ROWS_DEV, 0)
        fresh_kv = fresh_kv.reshape(ROWS_DEV, KVH, 2, HD).astype(jnp.float32)
        allowed = jnp.arange(span, dtype=jnp.int32)[None, :] < lengths[:, None]
        scores = jnp.einsum('rgqd,rsgd->rgqs', queries, cache_rows[:, :, :, 0, :]) * scaling
        scores = jnp.where(allowed[:, None, None, :], scores, NEG)
        own_score = jnp.einsum('rgqd,rgd->rgq', queries, fresh_kv[:, :, 0, :]) * scaling
        row_max = jnp.maximum(jnp.max(scores, axis=-1), own_score)
        weights = jnp.where(allowed[:, None, None, :], jnp.exp(scores - row_max[..., None]), 0.0)
        own_weight = jnp.exp(own_score - row_max)
        denominator = jnp.sum(weights, axis=-1) + own_weight
        rounded = lax.optimization_barrier(weights.astype(jnp.bfloat16)).astype(jnp.float32)
        own_rounded = lax.optimization_barrier(own_weight.astype(jnp.bfloat16)).astype(jnp.float32)
        weighted = jnp.einsum('rgqs,rsgd->rgqd', rounded, cache_rows[:, :, :, 1, :])
        weighted = weighted + own_rounded[..., None] * fresh_kv[:, :, None, 1, :]
        return (weighted / denominator[..., None]).astype(jnp.bfloat16).reshape(ROWS_DEV, QH * HD)

    dec_attn = lax.map(decode_block, jnp.arange(ROWS // ROWS_DEV, dtype=jnp.int32)).reshape(ROWS, QH * HD)
    decoded = jnp.dot(dec_attn, out_weight, preferred_element_type=jnp.float32).astype(jnp.bfloat16)
    return attended, decoded
```

```python
import functools
import math

import jax
import jax.numpy as jnp
from jax import lax
from jax.experimental import pallas as pl
from jax.experimental.pallas import tpu as pltpu
from jax.sharding import PartitionSpec as P

HD = 128
T = 512
H = 8
PAGE = 32
NEG = -1e30
BIG = 2.0**100
C = HD**-0.5 * math.log2(math.e)
RES = 256
INC = 32
MIB = 2**20


def dot_t(a, b):
    return lax.dot_general(a, b, (((1,), (1,)), ((), ())), preferred_element_type=jnp.float32)


def segment_starts(ends, t):
    start = jnp.zeros_like(t)
    for e in ends:
        start = jnp.maximum(start, jnp.where(t >= e, e, 0))
    return start


def source(s):
    return s // 4 * 2 + s % 2, s % 4 // 2


def prefill_kernel(kind, nblocks, first, last, info, *refs):
    nref = 1 + nblocks
    q_ref, kv_refs = refs[0], refs[1:nref]
    base = 0 if kind == "final" else first // 4 * 4
    count = 2 * nblocks
    if kind == "first":
        m_ref, l_ref, acc_ref, buf, vx, bias, sem = refs[nref:]
    elif kind == "middle":
        m_ref, l_in, acc_in, l_ref, acc_ref, buf, vx, bias, sem = refs[nref:]
    else:
        m_in, l_in, acc_in, o_ref, m_ref, l_ref, acc_ref, buf, vx, bias, sem, fail = refs[nref:]
    me = info[0]
    t0 = me * T
    e0 = info[1]
    e1 = e0 + info[2]
    e2 = e1 + info[3]
    ends = (e0, e1, e2)
    lo = segment_starts(ends, t0)
    hi = segment_starts(ends, t0 + T - 1)

    def block_of(s):
        c = s // 4
        return (me - 4 * c) ^ (s - 4 * c)

    def needed(s):
        j = block_of(s)
        return (j >= 0) & (j <= me) & (lo < (j + 1) * T)

    def fetch(a, b):
        for s in range(a, b):
            @pl.when(needed(s))
            def _():
                r, k = source(s - base)
                pltpu.make_async_copy(kv_refs[r].at[k], buf.at[s - base], sem.at[s - base]).start()

    def await_slot(s):
        pltpu.make_async_copy(kv_refs[0].at[0], buf.at[s - base], sem.at[s - base]).wait()

    def set_bias(j):
        u = j * T + lax.broadcasted_iota(jnp.int32, (T, T), 1)
        t = t0 + lax.broadcasted_iota(jnp.int32, (T, 1), 0)
        ok = (u <= t) & (u >= segment_starts(ends, t))
        bias[...] = jnp.where(ok, 0.0, NEG)

    def scores(h, k, masked):
        s = dot_t(q_ref[:, pl.ds(pl.multiple_of(h * HD, HD), HD)], k) * C
        return s + bias[...] if masked else s

    def max_block(s):
        set_bias(block_of(s))
        k = buf[s - base, :, :HD]

        @pl.loop(0, H)
        def _(h):
            x = jnp.max(scores(h, k, True), axis=1, keepdims=True)
            m_ref[h] = jnp.maximum(m_ref[h], jnp.broadcast_to(x, (T, HD)))

    def add_block(s, masked):
        k = buf[s - base, :, :HD]
        vx[:, :HD] = buf[s - base, :, HD:]
        v = vx[...]

        def rest(h, x):
            m = m_ref[h]
            p = jnp.exp2(x - jnp.concatenate([m] * (T // HD), axis=1))
            pv = jnp.dot(p.astype(jnp.bfloat16), v, preferred_element_type=jnp.float32)
            l_ref[h] += pv[:, HD:]
            acc_ref[h] += pv[:, :HD]

        @pl.loop(0, H // 4)
        def _(g):
            x = scores(g * 4, k, masked)
            for i in range(4):
                y = scores(g * 4 + i + 1, k, masked) if i < 3 else None
                rest(g * 4 + i, x)
                x = y

    def sweep(a, b, wait):
        @pl.loop(a, b)
        def _(s):
            @pl.when(needed(s))
            def _():
                if wait:
                    await_slot(s)
                j = block_of(s)
                masked = (j == me) | (hi > j * T)

                @pl.when(masked)
                def _():
                    set_bias(j)
                    add_block(s, True)

                @pl.when(jnp.logical_not(masked))
                def _():
                    add_block(s, False)

    def clear():
        l_ref[...] = jnp.zeros_like(l_ref)
        acc_ref[...] = jnp.zeros_like(acc_ref)

    fetch(first, last)
    vx[:, HD:] = jnp.ones((T, HD), jnp.bfloat16)
    if kind == "first":
        m_ref[...] = jnp.full_like(m_ref, NEG)
        clear()
        await_slot(0)
        max_block(0)
        sweep(0, 1, False)
        sweep(1, last, True)
        return
    if kind == "final":
        m_ref[...] = m_in[...]
    l_ref[...] = l_in[...]
    acc_ref[...] = acc_in[...]
    sweep(first, last, True)
    if kind == "final":
        fail[0] = jnp.where(jnp.max(jnp.where(l_ref[...] < BIG, 0.0, 1.0)) > 0.0, 1, 0)

        @pl.when(fail[0] == 1)
        def _():
            fetch(0, first)
            for s in range(first):
                @pl.when(needed(s))
                def _():
                    await_slot(s)
            clear()

            @pl.loop(0, count)
            def _(s):
                @pl.when(needed(s))
                def _():
                    max_block(s)

            sweep(0, count, False)

        for h in range(H):
            o_ref[:, h * HD : (h + 1) * HD] = (acc_ref[h] / l_ref[h]).astype(jnp.bfloat16)


def prefill_call(kind, first, last, info, q, blocks, state=()):
    count = 2 * len(blocks)
    carry = jax.ShapeDtypeStruct((H, T, HD), jnp.float32)
    vmem = pl.BlockSpec(memory_space=pltpu.VMEM)
    scratch = [
        pltpu.VMEM((count, T, 2 * HD), jnp.bfloat16),
        pltpu.VMEM((T, 2 * HD), jnp.bfloat16),
        pltpu.VMEM((T, T), jnp.float32),
        pltpu.SemaphoreType.DMA((count,)),
    ]
    if kind == "final":
        scratch = [pltpu.VMEM((H, T, HD), jnp.float32)] * 3 + scratch + [pltpu.SMEM((1,), jnp.int32)]
        out_shape, out_specs = jax.ShapeDtypeStruct((T, H * HD), jnp.bfloat16), vmem
    else:
        n = 3 if kind == "first" else 2
        out_shape, out_specs = [carry] * n, [vmem] * n
    work = last - first
    return pl.pallas_call(
        functools.partial(prefill_kernel, kind, len(blocks), first, last),
        out_shape=out_shape,
        in_specs=[pl.BlockSpec(memory_space=pltpu.SMEM), vmem]
        + [pl.BlockSpec(memory_space=pltpu.HBM)] * len(blocks)
        + [vmem] * len(state),
        out_specs=out_specs,
        scratch_shapes=scratch,
        compiler_params=pltpu.CompilerParams(vmem_limit_bytes=(20 if kind == "final" else 12) * MIB),
        cost_estimate=pl.CostEstimate(
            flops=work * H * T * T * HD * 8, bytes_accessed=8 * MIB, transcendentals=work * H * T * T
        ),
        name="prefill_" + kind,
    )(info, q, *blocks, *state)


R = H * PAGE
NP = 16


def page_counts(tab_ref, lma, lmb, first, groups):
    last = tab_ref[PAGE : PAGE + 1, :]

    @pl.loop(0, groups)
    def _(g):
        page = first + g * 32 + lax.broadcasted_iota(jnp.int32, (32, R), 0)
        n = jnp.zeros((32, R), jnp.float32)
        for j in range(32):
            n += jnp.where(tab_ref[j : j + 1, :] == page, 1.0, 0.0)
        fewer = n - jnp.where(page == last, 1.0, 0.0)
        at = pl.ds(pl.multiple_of(g * 32, 32), 32)
        lma[at, :] = jnp.where(n > 0.5, jnp.log2(jnp.maximum(n, 1.0)), NEG)
        lmb[at, :] = jnp.where(fewer > 0.5, jnp.log2(jnp.maximum(fewer, 1.0)), NEG)


def load_queries(q_ref, qs):
    for h in range(H):
        qs[h * PAGE : (h + 1) * PAGE, :] = q_ref[:, h * HD : (h + 1) * HD]


def page_scores(pool, b, q, within, lma, lmb, m):
    k = pool[pl.ds(b * NP, NP), :, :HD].reshape(NP * PAGE, HD)
    s = (dot_t(k, q) * C).reshape(NP, PAGE, R)
    at = pl.ds(pl.multiple_of(b * NP, NP), NP)
    a = (lma[at, :] - m)[:, None, :]
    return (s + jnp.where(within[None], a, (lmb[at, :] - m)[:, None, :])).reshape(NP * PAGE, R)


def pages_sum(pool, blocks, per, q, within, lma, lmb, m, l_ref, acc_ref):
    @pl.loop(0, blocks // per)
    def _(g):
        l = l_ref[...]
        acc = acc_ref[...]
        x = page_scores(pool, g * per, q, within, lma, lmb, m)
        for i in range(per):
            b = g * per + i
            y = page_scores(pool, b + 1, q, within, lma, lmb, m) if i < per - 1 else None
            v = pool[pl.ds(b * NP, NP), :, HD:].reshape(NP * PAGE, HD)
            p = jnp.exp2(x)
            l = l + jnp.sum(p, axis=0, keepdims=True)
            acc = acc + lax.dot_general(
                v, p.astype(jnp.bfloat16), (((0,), (0,)), ((), ())),
                preferred_element_type=jnp.float32,
            )
            x = y
        l_ref[...] = l
        acc_ref[...] = acc


def own_scores(new_ref, q):
    own = dot_t(new_ref[:, :HD], q) * C
    row = lax.broadcasted_iota(jnp.int32, (PAGE, R), 0)
    mine = row == (lax.broadcasted_iota(jnp.int32, (PAGE, R), 1) & (PAGE - 1))
    return jnp.where(mine, own, NEG)


def start_sums(new_ref, own, m, l_ref, acc_ref):
    p = jnp.exp2(own - m)
    l_ref[...] = jnp.sum(p, axis=0, keepdims=True)
    acc_ref[...] = lax.dot_general(
        new_ref[:, HD:], p.astype(jnp.bfloat16), (((0,), (0,)), ((), ())),
        preferred_element_type=jnp.float32,
    )


def rows_within(tab_ref):
    return lax.broadcasted_iota(jnp.int32, (PAGE, R), 0) < tab_ref[PAGE + 1 : PAGE + 2, :]


def resident_kernel(tab_ref, q_ref, new_ref, pool, m_ref, l_ref, acc_ref, lma, lmb, qs):
    load_queries(q_ref, qs)
    q = qs[...]
    own = own_scores(new_ref, q)
    m = jnp.max(own, axis=0, keepdims=True)
    m_ref[...] = m
    page_counts(tab_ref, lma, lmb, 0, RES // 32)
    start_sums(new_ref, own, m, l_ref, acc_ref)
    pages_sum(pool, RES // NP, 4, q, rows_within(tab_ref), lma, lmb, m, l_ref, acc_ref)


def handed_kernel(nblocks, ids, info, tab_ref, q_ref, new_ref, res_ref, m_in, l_in, acc_in, *refs):
    kv_refs = refs[:nblocks]
    o_ref, pool, qs, lma, lmb, rma, rmb, m_ref, l_ref, acc_ref, sem, fail = refs[nblocks:]
    me = info[0]
    pool[...] = jnp.zeros((INC, PAGE, 2 * HD), jnp.bfloat16)
    n_owned = ids[INC]

    @pl.loop(0, n_owned)
    def _(k):
        page = ids[k]
        j = page // 16
        c = (me // 4 - j // 4) & 3
        b = (me ^ j) & 3
        at = pl.ds(pl.multiple_of((page % 16) * PAGE, PAGE), PAGE)
        r = 2 * c + (b & 1)
        for i in range(nblocks):
            @pl.when(r == i)
            def _():
                pltpu.make_async_copy(kv_refs[i].at[b // 2, at], pool.at[k], sem.at[k]).start()

    load_queries(q_ref, qs)
    q = qs[...]
    within = rows_within(tab_ref)
    page_counts(tab_ref, lma, lmb, RES, INC // 32)
    m_ref[...] = m_in[...]
    l_ref[...] = l_in[...]
    acc_ref[...] = acc_in[...]

    @pl.loop(0, n_owned)
    def _(k):
        pltpu.make_async_copy(kv_refs[0].at[0, pl.ds(0, PAGE)], pool.at[k], sem.at[k]).wait()

    pages_sum(pool, INC // NP, 2, q, within, lma, lmb, m_in[...], l_ref, acc_ref)
    fail[0] = jnp.where(jnp.max(jnp.where(l_ref[...] < BIG, 0.0, 1.0)) > 0.0, 1, 0)

    @pl.when(fail[0] == 1)
    def _():
        page_counts(tab_ref, rma, rmb, 0, RES // 32)
        zero = jnp.zeros((1, R), jnp.float32)

        def raise_max(p, n, a, b):
            @pl.loop(0, n)
            def _(i):
                s = page_scores(p, i, q, within, a, b, zero)
                m_ref[...] = jnp.maximum(m_ref[...], jnp.max(s, axis=0, keepdims=True))

        raise_max(res_ref, RES // NP, rma, rmb)
        raise_max(pool, INC // NP, lma, lmb)
        m = m_ref[...]
        start_sums(new_ref, own_scores(new_ref, q), m, l_ref, acc_ref)
        pages_sum(res_ref, RES // NP, 1, q, within, rma, rmb, m, l_ref, acc_ref)
        pages_sum(pool, INC // NP, 1, q, within, lma, lmb, m, l_ref, acc_ref)

    o = (acc_ref[...] / l_ref[...]).T
    for h in range(H):
        o_ref[:, h * HD : (h + 1) * HD] = o[h * PAGE : (h + 1) * PAGE, :].astype(jnp.bfloat16)


SMEM_ALL = pl.BlockSpec(memory_space=pltpu.SMEM)
VMEM_ALL = pl.BlockSpec(memory_space=pltpu.VMEM)
HBM_ALL = pl.BlockSpec(memory_space=pltpu.HBM)


def row_shape(n):
    return jax.ShapeDtypeStruct((n, R), jnp.float32)


def resident_call(tab, dec_q, dec_new, resident):
    return pl.pallas_call(
        resident_kernel,
        out_shape=[row_shape(1), row_shape(1), row_shape(HD)],
        in_specs=[VMEM_ALL] * 4,
        out_specs=[VMEM_ALL] * 3,
        scratch_shapes=[
            pltpu.VMEM((RES, R), jnp.float32),
            pltpu.VMEM((RES, R), jnp.float32),
            pltpu.VMEM((R, HD), jnp.bfloat16),
        ],
        compiler_params=pltpu.CompilerParams(vmem_limit_bytes=12 * MIB),
        cost_estimate=pl.CostEstimate(
            flops=4 * R * 8192 * HD * 8, bytes_accessed=5 * MIB, transcendentals=R * 8192
        ),
        name="decode_resident",
    )(tab, dec_q, dec_new, resident)


def handed_call(ids, info, tab, dec_q, dec_new, resident, sums, blocks):
    n = len(blocks)
    return pl.pallas_call(
        functools.partial(handed_kernel, n),
        out_shape=jax.ShapeDtypeStruct((PAGE, H * HD), jnp.bfloat16),
        in_specs=[SMEM_ALL] * 2 + [VMEM_ALL] * 7 + [HBM_ALL] * n,
        out_specs=VMEM_ALL,
        scratch_shapes=[
            pltpu.VMEM((INC, PAGE, 2 * HD), jnp.bfloat16),
            pltpu.VMEM((R, HD), jnp.bfloat16),
            pltpu.VMEM((INC, R), jnp.float32),
            pltpu.VMEM((INC, R), jnp.float32),
            pltpu.VMEM((RES, R), jnp.float32),
            pltpu.VMEM((RES, R), jnp.float32),
            pltpu.VMEM((1, R), jnp.float32),
            pltpu.VMEM((1, R), jnp.float32),
            pltpu.VMEM((HD, R), jnp.float32),
            pltpu.SemaphoreType.DMA((INC,)),
            pltpu.SMEM((1,), jnp.int32),
        ],
        compiler_params=pltpu.CompilerParams(vmem_limit_bytes=12 * MIB),
        cost_estimate=pl.CostEstimate(
            flops=4 * R * 1024 * HD * 8, bytes_accessed=2 * MIB, transcendentals=R * 1024
        ),
        name="decode_handed",
    )(ids, info, tab, dec_q, dec_new, resident, *sums, *blocks)


def project_kernel(nblocks, info, w_ref, *refs):
    a_refs = refs[:nblocks]
    o_ref, rows = refs[nblocks:]
    me = info[0]
    for s in range(2 * nblocks):
        r, i = source(s)
        j = ((me - s // 4 * 4) ^ (s % 4)) & 15
        rows[pl.ds(pl.multiple_of(j * PAGE, PAGE), PAGE), :] = a_refs[r][i]
    o_ref[...] = jnp.dot(rows[...], w_ref[...], preferred_element_type=jnp.float32).astype(jnp.bfloat16)


def project_call(info, w, blocks):
    vmem = pl.BlockSpec(memory_space=pltpu.VMEM)
    return pl.pallas_call(
        functools.partial(project_kernel, len(blocks)),
        out_shape=jax.ShapeDtypeStruct((512, w.shape[1]), jnp.bfloat16),
        in_specs=[pl.BlockSpec(memory_space=pltpu.SMEM), vmem] + [vmem] * len(blocks),
        out_specs=vmem,
        scratch_shapes=[pltpu.VMEM((512, w.shape[0]), jnp.bfloat16)],
        compiler_params=pltpu.CompilerParams(vmem_limit_bytes=6 * MIB),
        cost_estimate=pl.CostEstimate(
            flops=2 * 512 * w.shape[0] * w.shape[1], bytes_accessed=3 * MIB, transcendentals=0
        ),
        name="project",
    )(info, w, *blocks)


def swap(x, bit):
    return lax.ppermute(x, "ctx", [(i, i ^ bit) for i in range(16)])


def turn(x, s):
    return lax.ppermute(x, "ctx", [(i, (i + 4 * s) % 16) for i in range(16)])


def after(x, y):
    return lax.optimization_barrier((x, y))[0]


def gather_ctx(x, z_gate=None, y_gate=None):
    x = x[None]
    z = swap(x, 2)
    if z_gate is not None:
        z = after(z, z_gate)
    pair = jnp.concatenate([x, z], axis=0)
    across = {s: turn(pair, s) for s in (1, 3, 2)}
    near = {0: swap(pair, 1)}
    across[0] = pair

    def finish(y_gate):
        for s in (1, 3, 2):
            if y_gate is not None:
                across[s] = after(across[s], y_gate)
            near[s] = swap(across[s], 1)
        return [a[s] for s in range(4) for a in (across, near)]

    return pair, near[0], finish


def shards(
    prompt_lens, pre_q, pre_kv, owners, resident, page_table, cache_len, dec_q, dec_new, out_weight
):
    me = lax.axis_index("ctx").astype(jnp.int32)
    info = jnp.concatenate([me[None], prompt_lens.astype(jnp.int32)])

    owned = owners == me
    at = jnp.arange(256, dtype=jnp.int32)
    rank = jnp.sum((owned[None, :] & (at[None, :] < at[:, None])).astype(jnp.int32), axis=1)
    hit = owned[None, :] & (rank[None, :] == jnp.arange(INC, dtype=jnp.int32)[:, None])
    ids = jnp.sum(jnp.where(hit, at[None, :], 0), axis=1)
    ids = jnp.concatenate([ids, jnp.sum(owned.astype(jnp.int32))[None]])

    slot = jnp.where(page_table < 4096, page_table - me * RES, page_table - 4096 + RES)
    col = jnp.arange(PAGE, dtype=jnp.int32)
    end = (cache_len - 1) // PAGE
    last = jnp.sum(jnp.where(col[None, :] == end[:, None], slot, 0), axis=1)
    rem = cache_len - end * PAGE
    slot = jnp.where(col[None, :] <= end[:, None], slot, -1)
    tab = jnp.concatenate([slot.T, last[None], rem[None], jnp.zeros((6, PAGE), jnp.int32)], axis=0)
    tab = jnp.tile(tab, (1, H))

    pair, near, finish = gather_ctx(pre_kv)
    sums = resident_call(after(tab, pair), dec_q, dec_new, resident)
    m, *state = prefill_call("first", 0, 4, after(info, sums[1]), pre_q, [pair, near])
    blocks = finish(state[0])
    dec = handed_call(ids, info, tab, dec_q, dec_new, resident, sums, blocks)
    state = prefill_call("middle", 4, 6, after(info, dec), pre_q, blocks[2:4], (m, *state))
    _, _, finish = gather_ctx(dec, state[0])
    state = prefill_call("middle", 6, 8, info, pre_q, blocks[2:4], (m, *state))
    part = project_call(info, out_weight, finish(state[0]))
    attended = prefill_call("final", 8, 16, after(info, part), pre_q, blocks, (m, *state))
    part = lax.all_to_all(part.reshape(8, 64, 512), "grp", split_axis=0, concat_axis=0, tiled=True)
    decoded = jnp.sum(part.astype(jnp.float32), axis=0).astype(jnp.bfloat16)
    return attended, decoded


def solution(mesh):
    return jax.shard_map(
        shards,
        mesh=mesh,
        in_specs=(
            P(),
            P("ctx", "grp"),
            P("ctx", "grp"),
            P(),
            P("ctx", None, "grp"),
            P("ctx", None),
            P("ctx"),
            P("ctx", "grp"),
            P("ctx", "grp"),
            P("grp", "ctx"),
        ),
        out_specs=(P("ctx", "grp"), P("grp", "ctx")),
        check_vma=False,
    )
```

```python
import functools
import math

import jax
import jax.numpy as jnp
from jax import lax
from jax.experimental import pallas as pl
from jax.experimental.pallas import tpu as pltpu
from jax.sharding import PartitionSpec as P

HD = 128
T = 512
H = 8
PAGE = 32
NEG = -1e30
BIG = 2.0**100
C = HD**-0.5 * math.log2(math.e)
RES = 256
INC = 32
MIB = 2**20


SMEM_ALL = pl.BlockSpec(memory_space=pltpu.SMEM)
VMEM_ALL = pl.BlockSpec(memory_space=pltpu.VMEM)
HBM_ALL = pl.BlockSpec(memory_space=pltpu.HBM)


def in_hbm(x):
    return pltpu.with_memory_space_constraint(x, pltpu.HBM)


def dot_t(a, b):
    return lax.dot_general(a, b, (((1,), (1,)), ((), ())), preferred_element_type=jnp.float32)


def segment_starts(ends, t):
    start = jnp.zeros_like(t)
    for e in ends:
        start = jnp.maximum(start, jnp.where(t >= e, e, 0))
    return start


def source(s):
    return s // 4 * 2 + s % 2, s % 4 // 2


def prefill_kernel(kind, nblocks, first, last, info, *refs):
    nref = 1 + nblocks
    q_ref, kv_refs = refs[0], refs[1:nref]
    base = 0 if kind == "final" else first // 4 * 4
    count = 2 * nblocks
    if kind == "first":
        m_ref, l_ref, acc_ref, buf, vx, start, row, bias, sem = refs[nref:]
    elif kind == "middle":
        m_ref, l_in, acc_in, l_ref, acc_ref, buf, vx, start, row, bias, sem = refs[nref:]
    else:
        m_in, l_in, acc_in, o_ref, m_ref, l_ref, acc_ref, q_buf = refs[nref : nref + 8]
        buf, vx, start, row, bias, sem, sem_in, fail = refs[nref + 8 :]
        moves = [
            pltpu.make_async_copy(a, b, sem_in.at[i])
            for i, (a, b) in enumerate(((q_ref, q_buf), (m_in, m_ref), (l_in, l_ref), (acc_in, acc_ref)))
        ]
        for c in moves:
            c.start()
        q_ref = q_buf
    me = info[0]
    t0 = me * T
    e0 = info[1]
    e1 = e0 + info[2]
    e2 = e1 + info[3]
    ends = (e0, e1, e2)
    lo = segment_starts(ends, t0)

    def block_of(s):
        c = s // 4
        return (me - 4 * c) ^ (s - 4 * c)

    def needed(s):
        j = block_of(s)
        return (j >= 0) & (j <= me) & (lo < (j + 1) * T)

    def fetch(a, b):
        for s in range(a, b):
            @pl.when(needed(s))
            def _():
                r, k = source(s - base)
                pltpu.make_async_copy(kv_refs[r].at[k], buf.at[s - base], sem.at[s - base]).start()

    def await_slot(s):
        pltpu.make_async_copy(kv_refs[0].at[0], buf.at[s - base], sem.at[s - base]).wait()

    def set_bias(j):
        u = j * T + lax.broadcasted_iota(jnp.int32, (T, T), 1)
        t = t0 + lax.broadcasted_iota(jnp.int32, (T, 1), 0)
        ok = (u <= t) & (u >= start[:, :1])
        bias[...] = jnp.where(ok, 0.0, NEG)

    def scores(h, k, masked):
        s = dot_t(q_ref[:, pl.ds(pl.multiple_of(h * HD, HD), HD)], k) * C
        return s + bias[...] if masked else s

    def max_block(s):
        set_bias(block_of(s))
        k = buf[s - base, :, :HD]

        @pl.loop(0, H)
        def _(h):
            x = jnp.max(scores(h, k, True), axis=1, keepdims=True)
            m_ref[h] = jnp.maximum(m_ref[h], jnp.broadcast_to(x, (T, HD)))

    def add_block(s, masked, fresh=False):
        k = buf[s - base, :, :HD]
        vx[:, :HD] = buf[s - base, :, HD:]
        v = vx[...]

        def rest(h, x):
            if fresh:
                m = jnp.broadcast_to(jnp.max(x, axis=1, keepdims=True), (T, HD))
                m_ref[h] = m
            else:
                m = m_ref[h] if masked else m_ref[h] + row[...]
            p = jnp.exp2(x - jnp.concatenate([m] * (T // HD), axis=1))
            pv = jnp.dot(p.astype(jnp.bfloat16), v, preferred_element_type=jnp.float32)
            if fresh:
                l_ref[h] = pv[:, HD:]
                acc_ref[h] = pv[:, :HD]
            else:
                l_ref[h] += pv[:, HD:]
                acc_ref[h] += pv[:, :HD]

        @pl.loop(0, H // 4)
        def _(g):
            x = scores(g * 4, k, masked)
            for i in range(4):
                y = scores(g * 4 + i + 1, k, masked) if i < 3 else None
                rest(g * 4 + i, x)
                x = y

    def sweep(a, b, wait):
        @pl.loop(a, b)
        def _(s):
            @pl.when(needed(s))
            def _():
                if wait:
                    await_slot(s)
                j = block_of(s)
                masked = j == me
                for e in ends:
                    masked |= (e > j * T) & (e < (j + 1) * T)

                @pl.when(masked)
                def _():
                    set_bias(j)
                    add_block(s, True)

                @pl.when(jnp.logical_not(masked))
                def _():
                    row[...] = jnp.where(start[...] >= (j + 1) * T, -NEG, 0.0)
                    add_block(s, False)

    def clear():
        l_ref[...] = jnp.zeros_like(l_ref)
        acc_ref[...] = jnp.zeros_like(acc_ref)

    fetch(first, last)
    start[...] = segment_starts(ends, t0 + lax.broadcasted_iota(jnp.int32, (T, HD), 0))
    vx[:, HD:] = jnp.ones((T, HD), jnp.bfloat16)
    if kind == "first":
        await_slot(0)
        set_bias(me)
        add_block(0, True, fresh=True)
        sweep(1, last, True)
        return
    if kind == "final":
        for c in moves:
            c.wait()
    else:
        l_ref[...] = l_in[...]
        acc_ref[...] = acc_in[...]
    sweep(first, last, True)
    if kind == "final":
        fail[0] = jnp.where(jnp.max(jnp.where(l_ref[...] < BIG, 0.0, 1.0)) > 0.0, 1, 0)

        @pl.when(fail[0] == 1)
        def _():
            fetch(0, first)
            for s in range(first):
                @pl.when(needed(s))
                def _():
                    await_slot(s)
            clear()

            @pl.loop(0, count)
            def _(s):
                @pl.when(needed(s))
                def _():
                    max_block(s)

            sweep(0, count, False)

        for h in range(H):
            o_ref[:, h * HD : (h + 1) * HD] = (acc_ref[h] / l_ref[h]).astype(jnp.bfloat16)


def prefill_call(kind, first, last, info, q, blocks, state=()):
    count = 2 * len(blocks)
    carry = jax.ShapeDtypeStruct((H, T, HD), jnp.float32)
    vmem = pl.BlockSpec(memory_space=pltpu.VMEM)
    scratch = [
        pltpu.VMEM((count, T, 2 * HD), jnp.bfloat16),
        pltpu.VMEM((T, 2 * HD), jnp.bfloat16),
        pltpu.VMEM((T, HD), jnp.int32),
        pltpu.VMEM((T, HD), jnp.float32),
        pltpu.VMEM((T, T), jnp.float32),
        pltpu.SemaphoreType.DMA((count,)),
    ]
    if kind == "final":
        scratch = (
            [pltpu.VMEM((H, T, HD), jnp.float32)] * 3
            + [pltpu.VMEM((T, H * HD), jnp.bfloat16)]
            + scratch
            + [pltpu.SemaphoreType.DMA((4,)), pltpu.SMEM((1,), jnp.int32)]
        )
        out_shape, out_specs = jax.ShapeDtypeStruct((T, H * HD), jnp.bfloat16), vmem
    else:
        n = 3 if kind == "first" else 2
        out_shape, out_specs = [carry] * n, [vmem] * n
    work = last - first
    blocks = [in_hbm(b) for b in blocks]
    data = vmem
    if kind == "final":
        q, state, data = in_hbm(q), [in_hbm(x) for x in state], HBM_ALL
    return pl.pallas_call(
        functools.partial(prefill_kernel, kind, len(blocks), first, last),
        out_shape=out_shape,
        in_specs=[SMEM_ALL, data] + [HBM_ALL] * len(blocks) + [data] * len(state),
        out_specs=out_specs,
        scratch_shapes=scratch,
        compiler_params=pltpu.CompilerParams(vmem_limit_bytes=(22 if kind == "final" else 12) * MIB),
        cost_estimate=pl.CostEstimate(
            flops=work * H * T * T * HD * 8, bytes_accessed=8 * MIB, transcendentals=work * H * T * T
        ),
        name="prefill_" + kind,
    )(info, q, *blocks, *state)


R = H * PAGE
NP = 16


def page_counts(tab_ref, lma, lmb, first, groups):
    last = tab_ref[PAGE : PAGE + 1, :]

    @pl.loop(0, groups)
    def _(g):
        page = first + g * 32 + lax.broadcasted_iota(jnp.int32, (32, R), 0)
        n = jnp.zeros((32, R), jnp.float32)
        for j in range(32):
            n += jnp.where(tab_ref[j : j + 1, :] == page, 1.0, 0.0)
        fewer = n - jnp.where(page == last, 1.0, 0.0)
        at = pl.ds(pl.multiple_of(g * 32, 32), 32)
        lma[at, :] = jnp.where(n > 0.5, jnp.log2(jnp.maximum(n, 1.0)), NEG)
        lmb[at, :] = jnp.where(fewer > 0.5, jnp.log2(jnp.maximum(fewer, 1.0)), NEG)


def load_queries(q_ref, qs):
    for h in range(H):
        qs[h * PAGE : (h + 1) * PAGE, :] = q_ref[:, h * HD : (h + 1) * HD]


def page_scores(pool, b, q, within, lma, lmb, m):
    k = pool[pl.ds(b * NP, NP), :, :HD].reshape(NP * PAGE, HD)
    s = (dot_t(k, q) * C).reshape(NP, PAGE, R)
    at = pl.ds(pl.multiple_of(b * NP, NP), NP)
    a = (lma[at, :] - m)[:, None, :]
    return (s + jnp.where(within[None], a, (lmb[at, :] - m)[:, None, :])).reshape(NP * PAGE, R)


def pages_sum(pool, blocks, per, q, within, lma, lmb, m, l_ref, acc_ref):
    @pl.loop(0, blocks // per)
    def _(g):
        l = l_ref[...]
        acc = acc_ref[...]
        x = page_scores(pool, g * per, q, within, lma, lmb, m)
        for i in range(per):
            b = g * per + i
            y = page_scores(pool, b + 1, q, within, lma, lmb, m) if i < per - 1 else None
            v = pool[pl.ds(b * NP, NP), :, HD:].reshape(NP * PAGE, HD)
            p = jnp.exp2(x)
            l = l + jnp.sum(p, axis=0, keepdims=True)
            acc = acc + lax.dot_general(
                v, p.astype(jnp.bfloat16), (((0,), (0,)), ((), ())),
                preferred_element_type=jnp.float32,
            )
            x = y
        l_ref[...] = l
        acc_ref[...] = acc


def own_scores(new_ref, q):
    own = dot_t(new_ref[:, :HD], q) * C
    row = lax.broadcasted_iota(jnp.int32, (PAGE, R), 0)
    mine = row == (lax.broadcasted_iota(jnp.int32, (PAGE, R), 1) & (PAGE - 1))
    return jnp.where(mine, own, NEG)


def start_sums(new_ref, own, m, l_ref, acc_ref):
    p = jnp.exp2(own - m)
    l_ref[...] = jnp.sum(p, axis=0, keepdims=True)
    acc_ref[...] = lax.dot_general(
        new_ref[:, HD:], p.astype(jnp.bfloat16), (((0,), (0,)), ((), ())),
        preferred_element_type=jnp.float32,
    )


def rows_within(tab_ref):
    return lax.broadcasted_iota(jnp.int32, (PAGE, R), 0) < tab_ref[PAGE + 1 : PAGE + 2, :]


def resident_kernel(tab_ref, q_ref, new_ref, pool, m_ref, l_ref, acc_ref, lma, lmb, qs):
    load_queries(q_ref, qs)
    q = qs[...]
    own = own_scores(new_ref, q)
    m = jnp.max(own, axis=0, keepdims=True)
    m_ref[...] = m
    page_counts(tab_ref, lma, lmb, 0, RES // 32)
    start_sums(new_ref, own, m, l_ref, acc_ref)
    pages_sum(pool, RES // NP, 4, q, rows_within(tab_ref), lma, lmb, m, l_ref, acc_ref)


def handed_kernel(nblocks, ids, info, tab_ref, q_ref, new_ref, res_ref, m_in, l_in, acc_in, *refs):
    kv_refs = refs[:nblocks]
    o_ref, pool, qs, lma, lmb, rma, rmb, res, m_ref, l_ref, acc_ref, sem, fail = refs[nblocks:]
    me = info[0]
    pool[...] = jnp.zeros((INC, PAGE, 2 * HD), jnp.bfloat16)
    n_owned = ids[INC]

    @pl.loop(0, n_owned)
    def _(k):
        page = ids[k]
        j = page // 16
        c = (me // 4 - j // 4) & 3
        b = (me ^ j) & 3
        at = pl.ds(pl.multiple_of((page % 16) * PAGE, PAGE), PAGE)
        r = 2 * c + (b & 1)
        for i in range(nblocks):
            @pl.when(r == i)
            def _():
                pltpu.make_async_copy(kv_refs[i].at[b // 2, at], pool.at[k], sem.at[k]).start()

    load_queries(q_ref, qs)
    q = qs[...]
    within = rows_within(tab_ref)
    page_counts(tab_ref, lma, lmb, RES, INC // 32)
    m_ref[...] = m_in[...]
    l_ref[...] = l_in[...]
    acc_ref[...] = acc_in[...]

    @pl.loop(0, n_owned)
    def _(k):
        pltpu.make_async_copy(kv_refs[0].at[0, pl.ds(0, PAGE)], pool.at[k], sem.at[k]).wait()

    pages_sum(pool, INC // NP, 2, q, within, lma, lmb, m_in[...], l_ref, acc_ref)
    fail[0] = jnp.where(jnp.max(jnp.where(l_ref[...] < BIG, 0.0, 1.0)) > 0.0, 1, 0)

    @pl.when(fail[0] == 1)
    def _():
        copy = pltpu.make_async_copy(res_ref, res, sem.at[0])
        copy.start()
        page_counts(tab_ref, rma, rmb, 0, RES // 32)
        copy.wait()
        zero = jnp.zeros((1, R), jnp.float32)

        def raise_max(p, n, a, b):
            @pl.loop(0, n)
            def _(i):
                s = page_scores(p, i, q, within, a, b, zero)
                m_ref[...] = jnp.maximum(m_ref[...], jnp.max(s, axis=0, keepdims=True))

        raise_max(res, RES // NP, rma, rmb)
        raise_max(pool, INC // NP, lma, lmb)
        m = m_ref[...]
        start_sums(new_ref, own_scores(new_ref, q), m, l_ref, acc_ref)
        pages_sum(res, RES // NP, 1, q, within, rma, rmb, m, l_ref, acc_ref)
        pages_sum(pool, INC // NP, 1, q, within, lma, lmb, m, l_ref, acc_ref)

    o = (acc_ref[...] / l_ref[...]).T
    for h in range(H):
        o_ref[:, h * HD : (h + 1) * HD] = o[h * PAGE : (h + 1) * PAGE, :].astype(jnp.bfloat16)


def row_shape(n):
    return jax.ShapeDtypeStruct((n, R), jnp.float32)


def resident_call(tab, dec_q, dec_new, resident):
    return pl.pallas_call(
        resident_kernel,
        out_shape=[row_shape(1), row_shape(1), row_shape(HD)],
        in_specs=[VMEM_ALL] * 4,
        out_specs=[VMEM_ALL] * 3,
        scratch_shapes=[
            pltpu.VMEM((RES, R), jnp.float32),
            pltpu.VMEM((RES, R), jnp.float32),
            pltpu.VMEM((R, HD), jnp.bfloat16),
        ],
        compiler_params=pltpu.CompilerParams(vmem_limit_bytes=12 * MIB),
        cost_estimate=pl.CostEstimate(
            flops=4 * R * 8192 * HD * 8, bytes_accessed=5 * MIB, transcendentals=R * 8192
        ),
        name="decode_resident",
    )(tab, dec_q, dec_new, resident)


def handed_call(ids, info, tab, dec_q, dec_new, resident, sums, blocks):
    n = len(blocks)
    return pl.pallas_call(
        functools.partial(handed_kernel, n),
        out_shape=jax.ShapeDtypeStruct((PAGE, H * HD), jnp.bfloat16),
        in_specs=[SMEM_ALL] * 2 + [VMEM_ALL] * 3 + [HBM_ALL] + [VMEM_ALL] * 3 + [HBM_ALL] * n,
        out_specs=VMEM_ALL,
        scratch_shapes=[
            pltpu.VMEM((INC, PAGE, 2 * HD), jnp.bfloat16),
            pltpu.VMEM((R, HD), jnp.bfloat16),
            pltpu.VMEM((INC, R), jnp.float32),
            pltpu.VMEM((INC, R), jnp.float32),
            pltpu.VMEM((RES, R), jnp.float32),
            pltpu.VMEM((RES, R), jnp.float32),
            pltpu.VMEM((RES, PAGE, 2 * HD), jnp.bfloat16),
            pltpu.VMEM((1, R), jnp.float32),
            pltpu.VMEM((1, R), jnp.float32),
            pltpu.VMEM((HD, R), jnp.float32),
            pltpu.SemaphoreType.DMA((INC,)),
            pltpu.SMEM((1,), jnp.int32),
        ],
        compiler_params=pltpu.CompilerParams(vmem_limit_bytes=12 * MIB),
        cost_estimate=pl.CostEstimate(
            flops=4 * R * 1024 * HD * 8, bytes_accessed=2 * MIB, transcendentals=R * 1024
        ),
        name="decode_handed",
    )(ids, info, tab, dec_q, dec_new, in_hbm(resident), *sums, *[in_hbm(b) for b in blocks])


def project_kernel(nblocks, info, w_ref, *refs):
    a_refs = refs[:nblocks]
    o_ref, rows = refs[nblocks:]
    me = info[0]
    for s in range(2 * nblocks):
        r, i = source(s)
        j = ((me - s // 4 * 4) ^ (s % 4)) & 15
        rows[pl.ds(pl.multiple_of(j * PAGE, PAGE), PAGE), :] = a_refs[r][i]
    o_ref[...] = jnp.dot(rows[...], w_ref[...], preferred_element_type=jnp.float32).astype(jnp.bfloat16)


def project_call(info, w, blocks):
    vmem = pl.BlockSpec(memory_space=pltpu.VMEM)
    return pl.pallas_call(
        functools.partial(project_kernel, len(blocks)),
        out_shape=jax.ShapeDtypeStruct((512, w.shape[1]), jnp.bfloat16),
        in_specs=[pl.BlockSpec(memory_space=pltpu.SMEM), vmem] + [vmem] * len(blocks),
        out_specs=vmem,
        scratch_shapes=[pltpu.VMEM((512, w.shape[0]), jnp.bfloat16)],
        compiler_params=pltpu.CompilerParams(vmem_limit_bytes=6 * MIB),
        cost_estimate=pl.CostEstimate(
            flops=2 * 512 * w.shape[0] * w.shape[1], bytes_accessed=3 * MIB, transcendentals=0
        ),
        name="project",
    )(info, w, *blocks)


def swap(x, bit):
    return lax.ppermute(x, "ctx", [(i, i ^ bit) for i in range(16)])


def turn(x, s):
    return lax.ppermute(x, "ctx", [(i, (i + 4 * s) % 16) for i in range(16)])


def after(x, y):
    return lax.optimization_barrier((x, y))[0]


def gather_ctx(x, z_gate=None, y_gate=None):
    x = x[None]
    z = swap(x, 2)
    if z_gate is not None:
        z = after(z, z_gate)
    pair = jnp.concatenate([x, z], axis=0)
    across = {s: turn(pair, s) for s in (1, 3, 2)}
    near = {0: swap(pair, 1)}
    across[0] = pair

    def finish(y_gate):
        for s in (1, 3, 2):
            if y_gate is not None:
                across[s] = after(across[s], y_gate)
            near[s] = swap(across[s], 1)
        return [a[s] for s in range(4) for a in (across, near)]

    return pair, near[0], finish


def shards(
    prompt_lens, pre_q, pre_kv, owners, resident, page_table, cache_len, dec_q, dec_new, out_weight
):
    me = lax.axis_index("ctx").astype(jnp.int32)
    info = jnp.concatenate([me[None], prompt_lens.astype(jnp.int32)])

    owned = owners == me
    at = jnp.arange(256, dtype=jnp.int32)
    rank = jnp.sum((owned[None, :] & (at[None, :] < at[:, None])).astype(jnp.int32), axis=1)
    hit = owned[None, :] & (rank[None, :] == jnp.arange(INC, dtype=jnp.int32)[:, None])
    ids = jnp.sum(jnp.where(hit, at[None, :], 0), axis=1)
    ids = jnp.concatenate([ids, jnp.sum(owned.astype(jnp.int32))[None]])

    slot = jnp.where(page_table < 4096, page_table - me * RES, page_table - 4096 + RES)
    col = jnp.arange(PAGE, dtype=jnp.int32)
    end = (cache_len - 1) // PAGE
    last = jnp.sum(jnp.where(col[None, :] == end[:, None], slot, 0), axis=1)
    rem = cache_len - end * PAGE
    slot = jnp.where(col[None, :] <= end[:, None], slot, -1)
    tab = jnp.concatenate([slot.T, last[None], rem[None], jnp.zeros((6, PAGE), jnp.int32)], axis=0)
    tab = jnp.tile(tab, (1, H))

    pair, near, finish = gather_ctx(pre_kv)
    sums = resident_call(after(tab, pair), dec_q, dec_new, resident)
    m, *state = prefill_call("first", 0, 4, after(info, sums[1]), pre_q, [pair, near])
    blocks = finish(state[0])
    dec = handed_call(ids, info, tab, dec_q, dec_new, resident, sums, blocks)
    state = prefill_call("middle", 4, 6, after(info, dec), pre_q, blocks[2:4], (m, *state))
    _, _, finish = gather_ctx(dec, state[0])
    state = prefill_call("middle", 6, 8, info, pre_q, blocks[2:4], (m, *state))
    part = project_call(info, out_weight, finish(state[0]))
    attended = prefill_call("final", 8, 16, after(info, part), pre_q, blocks, (m, *state))
    part = lax.all_to_all(part.reshape(8, 64, 512), "grp", split_axis=0, concat_axis=0, tiled=True)
    decoded = jnp.sum(part.astype(jnp.float32), axis=0).astype(jnp.bfloat16)
    return attended, decoded


def solution(mesh):
    return jax.shard_map(
        shards,
        mesh=mesh,
        in_specs=(
            P(),
            P("ctx", "grp"),
            P("ctx", "grp"),
            P(),
            P("ctx", None, "grp"),
            P("ctx", None),
            P("ctx"),
            P("ctx", "grp"),
            P("ctx", "grp"),
            P("grp", "ctx"),
        ),
        out_specs=(P("ctx", "grp"), P("grp", "ctx")),
        check_vma=False,
    )
```

```python
import functools
import math

import jax
import jax.numpy as jnp
from jax import lax
from jax.experimental import pallas as pl
from jax.experimental.pallas import tpu as pltpu
from jax.sharding import PartitionSpec as P

HD = 128
T = 512
H = 8
PAGE = 32
NEG = -1e30
BIG = 2.0**100
C = HD**-0.5 * math.log2(math.e)
RES = 256
INC = 32
FIRST = 4
MIB = 2**20


SMEM_ALL = pl.BlockSpec(memory_space=pltpu.SMEM)
VMEM_ALL = pl.BlockSpec(memory_space=pltpu.VMEM)
HBM_ALL = pl.BlockSpec(memory_space=pltpu.HBM)


def in_hbm(x):
    return pltpu.with_memory_space_constraint(x, pltpu.HBM)


def dot_t(a, b):
    return lax.dot_general(a, b, (((1,), (1,)), ((), ())), preferred_element_type=jnp.float32)


def segment_starts(ends, t):
    start = jnp.zeros_like(t)
    for e in ends:
        start = jnp.maximum(start, jnp.where(t >= e, e, 0))
    return start


def source(s):
    return s // 4 * 2 + s % 2, s % 4 // 2


def prefill_kernel(kind, nblocks, first, last, info, *refs):
    nref = 1 + nblocks
    q_ref, kv_refs = refs[0], refs[1:nref]
    count = 2 * nblocks
    if kind == "first":
        m_ref, l_ref, acc_ref, buf, vx, start, row, bias, sem, use = refs[nref:]
    elif kind == "middle":
        m_ref, l_in, acc_in, l_ref, acc_ref, buf, vx, start, row, bias, sem, use = refs[nref:]
    else:
        m_in, l_in, acc_in, o_ref, m_ref, l_ref, acc_ref, q_buf = refs[nref : nref + 8]
        buf, vx, start, row, bias, sem, use, sem_in, fail = refs[nref + 8 :]
        moves = [
            pltpu.make_async_copy(a, b, sem_in.at[i])
            for i, (a, b) in enumerate(((q_ref, q_buf), (m_in, m_ref), (l_in, l_ref), (acc_in, acc_ref)))
        ]
        for c in moves:
            c.start()
        q_ref = q_buf
    me = info[0]
    t0 = me * T
    e0 = info[1]
    e1 = e0 + info[2]
    e2 = e1 + info[3]
    ends = (e0, e1, e2)
    lo = segment_starts(ends, t0)

    def block_of(s):
        c = s // 4
        return (me - 4 * c) ^ (s - 4 * c)

    def needed(s):
        j = block_of(s)
        return (j >= 0) & (j <= me) & (lo < (j + 1) * T)

    def choose(a, b):
        number = jnp.int32(0)
        for s in range(count):
            n = needed(s)
            use[s] = jnp.where(n & (number >= a) & (number < b), 1, 0)
            number += n.astype(jnp.int32)

    def fetch():
        for s in range(count):
            @pl.when(use[s] == 1)
            def _():
                r, k = source(s)
                pltpu.make_async_copy(kv_refs[r].at[k], buf.at[s], sem.at[s]).start()

    def await_slot(s):
        pltpu.make_async_copy(kv_refs[0].at[0], buf.at[s], sem.at[s]).wait()

    def set_bias(j):
        u = j * T + lax.broadcasted_iota(jnp.int32, (T, T), 1)
        t = t0 + lax.broadcasted_iota(jnp.int32, (T, 1), 0)
        ok = (u <= t) & (u >= start[:, :1])
        bias[...] = jnp.where(ok, 0.0, NEG)

    def scores(h, k, masked):
        s = dot_t(q_ref[:, pl.ds(pl.multiple_of(h * HD, HD), HD)], k) * C
        return s + bias[...] if masked else s

    def max_block(s):
        set_bias(block_of(s))
        k = buf[s, :, :HD]

        @pl.loop(0, H)
        def _(h):
            x = jnp.max(scores(h, k, True), axis=1, keepdims=True)
            m_ref[h] = jnp.maximum(m_ref[h], jnp.broadcast_to(x, (T, HD)))

    def add_block(s, masked, fresh=False):
        k = buf[s, :, :HD]
        vx[:, :HD] = buf[s, :, HD:]
        v = vx[...]

        def rest(h, x):
            if fresh:
                m = jnp.broadcast_to(jnp.max(x, axis=1, keepdims=True), (T, HD))
                m_ref[h] = m
            else:
                m = m_ref[h] if masked else m_ref[h] + row[...]
            p = jnp.exp2(x - jnp.concatenate([m] * (T // HD), axis=1))
            pv = jnp.dot(p.astype(jnp.bfloat16), v, preferred_element_type=jnp.float32)
            if fresh:
                l_ref[h] = pv[:, HD:]
                acc_ref[h] = pv[:, :HD]
            else:
                l_ref[h] += pv[:, HD:]
                acc_ref[h] += pv[:, :HD]

        @pl.loop(0, H // 4)
        def _(g):
            x = scores(g * 4, k, masked)
            for i in range(4):
                y = scores(g * 4 + i + 1, k, masked) if i < 3 else None
                rest(g * 4 + i, x)
                x = y

    def sweep(a, b, wait):
        @pl.loop(a, b)
        def _(s):
            @pl.when(use[s] == 1)
            def _():
                if wait:
                    await_slot(s)
                j = block_of(s)
                masked = j == me
                for e in ends:
                    masked |= (e > j * T) & (e < (j + 1) * T)

                @pl.when(masked)
                def _():
                    set_bias(j)
                    add_block(s, True)

                @pl.when(jnp.logical_not(masked))
                def _():
                    row[...] = jnp.where(start[...] >= (j + 1) * T, -NEG, 0.0)
                    add_block(s, False)

    def clear():
        l_ref[...] = jnp.zeros_like(l_ref)
        acc_ref[...] = jnp.zeros_like(acc_ref)

    choose(first, last)
    fetch()
    start[...] = segment_starts(ends, t0 + lax.broadcasted_iota(jnp.int32, (T, HD), 0))
    vx[:, HD:] = jnp.ones((T, HD), jnp.bfloat16)
    if kind == "first":
        await_slot(0)
        set_bias(me)
        add_block(0, True, fresh=True)
        sweep(1, count, True)
        return
    if kind == "final":
        for c in moves:
            c.wait()
    else:
        l_ref[...] = l_in[...]
        acc_ref[...] = acc_in[...]
    sweep(0, count, True)
    if kind == "final":
        fail[0] = jnp.where(jnp.max(jnp.where(l_ref[...] < BIG, 0.0, 1.0)) > 0.0, 1, 0)

        @pl.when(fail[0] == 1)
        def _():
            choose(0, first)
            fetch()

            @pl.loop(0, count)
            def _(s):
                @pl.when(use[s] == 1)
                def _():
                    await_slot(s)

            clear()
            choose(0, count)

            @pl.loop(0, count)
            def _(s):
                @pl.when(use[s] == 1)
                def _():
                    max_block(s)

            sweep(0, count, False)

        for h in range(H):
            o_ref[:, h * HD : (h + 1) * HD] = (acc_ref[h] / l_ref[h]).astype(jnp.bfloat16)


def prefill_call(kind, first, last, info, q, blocks, state=()):
    count = 2 * len(blocks)
    carry = jax.ShapeDtypeStruct((H, T, HD), jnp.float32)
    vmem = pl.BlockSpec(memory_space=pltpu.VMEM)
    scratch = [
        pltpu.VMEM((count, T, 2 * HD), jnp.bfloat16),
        pltpu.VMEM((T, 2 * HD), jnp.bfloat16),
        pltpu.VMEM((T, HD), jnp.int32),
        pltpu.VMEM((T, HD), jnp.float32),
        pltpu.VMEM((T, T), jnp.float32),
        pltpu.SemaphoreType.DMA((count,)),
        pltpu.SMEM((count,), jnp.int32),
    ]
    if kind == "final":
        scratch = (
            [pltpu.VMEM((H, T, HD), jnp.float32)] * 3
            + [pltpu.VMEM((T, H * HD), jnp.bfloat16)]
            + scratch
            + [pltpu.SemaphoreType.DMA((4,)), pltpu.SMEM((1,), jnp.int32)]
        )
        out_shape, out_specs = jax.ShapeDtypeStruct((T, H * HD), jnp.bfloat16), vmem
    else:
        n = 3 if kind == "first" else 2
        out_shape, out_specs = [carry] * n, [vmem] * n
    work = last - first
    blocks = [in_hbm(b) for b in blocks]
    data = vmem
    if kind == "final":
        q, state, data = in_hbm(q), [in_hbm(x) for x in state], HBM_ALL
    return pl.pallas_call(
        functools.partial(prefill_kernel, kind, len(blocks), first, last),
        out_shape=out_shape,
        in_specs=[SMEM_ALL, data] + [HBM_ALL] * len(blocks) + [data] * len(state),
        out_specs=out_specs,
        scratch_shapes=scratch,
        compiler_params=pltpu.CompilerParams(vmem_limit_bytes=(22 if kind == "final" else 14) * MIB),
        cost_estimate=pl.CostEstimate(
            flops=work * H * T * T * HD * 8, bytes_accessed=8 * MIB, transcendentals=work * H * T * T
        ),
        name="prefill_" + kind,
    )(info, q, *blocks, *state)


R = H * PAGE
NP = 16


def page_counts(tab_ref, lma, lmb, first, groups):
    last = tab_ref[PAGE : PAGE + 1, :]

    @pl.loop(0, groups)
    def _(g):
        page = first + g * 32 + lax.broadcasted_iota(jnp.int32, (32, R), 0)
        n = jnp.zeros((32, R), jnp.float32)
        for j in range(32):
            n += jnp.where(tab_ref[j : j + 1, :] == page, 1.0, 0.0)
        fewer = n - jnp.where(page == last, 1.0, 0.0)
        at = pl.ds(pl.multiple_of(g * 32, 32), 32)
        lma[at, :] = jnp.where(n > 0.5, jnp.log2(jnp.maximum(n, 1.0)), NEG)
        lmb[at, :] = jnp.where(fewer > 0.5, jnp.log2(jnp.maximum(fewer, 1.0)), NEG)


def load_queries(q_ref, qs):
    for h in range(H):
        qs[h * PAGE : (h + 1) * PAGE, :] = q_ref[:, h * HD : (h + 1) * HD]


def page_scores(pool, b, q, within, lma, lmb, m):
    k = pool[pl.ds(b * NP, NP), :, :HD].reshape(NP * PAGE, HD)
    s = (dot_t(k, q) * C).reshape(NP, PAGE, R)
    at = pl.ds(pl.multiple_of(b * NP, NP), NP)
    a = (lma[at, :] - m)[:, None, :]
    return (s + jnp.where(within[None], a, (lmb[at, :] - m)[:, None, :])).reshape(NP * PAGE, R)


def pages_sum(pool, blocks, per, q, within, lma, lmb, m, l_ref, acc_ref):
    @pl.loop(0, blocks // per)
    def _(g):
        l = l_ref[...]
        acc = acc_ref[...]
        x = page_scores(pool, g * per, q, within, lma, lmb, m)
        for i in range(per):
            b = g * per + i
            y = page_scores(pool, b + 1, q, within, lma, lmb, m) if i < per - 1 else None
            v = pool[pl.ds(b * NP, NP), :, HD:].reshape(NP * PAGE, HD)
            p = jnp.exp2(x)
            l = l + jnp.sum(p, axis=0, keepdims=True)
            acc = acc + lax.dot_general(
                v, p.astype(jnp.bfloat16), (((0,), (0,)), ((), ())),
                preferred_element_type=jnp.float32,
            )
            x = y
        l_ref[...] = l
        acc_ref[...] = acc


def own_scores(new_ref, q):
    own = dot_t(new_ref[:, :HD], q) * C
    row = lax.broadcasted_iota(jnp.int32, (PAGE, R), 0)
    mine = row == (lax.broadcasted_iota(jnp.int32, (PAGE, R), 1) & (PAGE - 1))
    return jnp.where(mine, own, NEG)


def start_sums(new_ref, own, m, l_ref, acc_ref):
    p = jnp.exp2(own - m)
    l_ref[...] = jnp.sum(p, axis=0, keepdims=True)
    acc_ref[...] = lax.dot_general(
        new_ref[:, HD:], p.astype(jnp.bfloat16), (((0,), (0,)), ((), ())),
        preferred_element_type=jnp.float32,
    )


def rows_within(tab_ref):
    return lax.broadcasted_iota(jnp.int32, (PAGE, R), 0) < tab_ref[PAGE + 1 : PAGE + 2, :]


def resident_kernel(tab_ref, q_ref, new_ref, pool, m_ref, l_ref, acc_ref, lma, lmb, qs):
    load_queries(q_ref, qs)
    q = qs[...]
    own = own_scores(new_ref, q)
    m = jnp.max(own, axis=0, keepdims=True)
    m_ref[...] = m
    page_counts(tab_ref, lma, lmb, 0, RES // 32)
    start_sums(new_ref, own, m, l_ref, acc_ref)
    pages_sum(pool, RES // NP, 4, q, rows_within(tab_ref), lma, lmb, m, l_ref, acc_ref)


def handed_kernel(nblocks, ids, info, tab_ref, q_ref, new_ref, res_ref, m_in, l_in, acc_in, *refs):
    kv_refs = refs[:nblocks]
    o_ref, pool, qs, lma, lmb, rma, rmb, res, m_ref, l_ref, acc_ref, sem, fail = refs[nblocks:]
    me = info[0]
    pool[...] = jnp.zeros((INC, PAGE, 2 * HD), jnp.bfloat16)
    n_owned = ids[INC]

    @pl.loop(0, n_owned)
    def _(k):
        page = ids[k]
        j = page // 16
        c = (me // 4 - j // 4) & 3
        b = (me ^ j) & 3
        at = pl.ds(pl.multiple_of((page % 16) * PAGE, PAGE), PAGE)
        r = 2 * c + (b & 1)
        for i in range(nblocks):
            @pl.when(r == i)
            def _():
                pltpu.make_async_copy(kv_refs[i].at[b // 2, at], pool.at[k], sem.at[k]).start()

    load_queries(q_ref, qs)
    q = qs[...]
    within = rows_within(tab_ref)
    page_counts(tab_ref, lma, lmb, RES, INC // 32)
    m_ref[...] = m_in[...]
    l_ref[...] = l_in[...]
    acc_ref[...] = acc_in[...]

    @pl.loop(0, n_owned)
    def _(k):
        pltpu.make_async_copy(kv_refs[0].at[0, pl.ds(0, PAGE)], pool.at[k], sem.at[k]).wait()

    pages_sum(pool, INC // NP, 2, q, within, lma, lmb, m_in[...], l_ref, acc_ref)
    fail[0] = jnp.where(jnp.max(jnp.where(l_ref[...] < BIG, 0.0, 1.0)) > 0.0, 1, 0)

    @pl.when(fail[0] == 1)
    def _():
        copy = pltpu.make_async_copy(res_ref, res, sem.at[0])
        copy.start()
        page_counts(tab_ref, rma, rmb, 0, RES // 32)
        copy.wait()
        zero = jnp.zeros((1, R), jnp.float32)

        def raise_max(p, n, a, b):
            @pl.loop(0, n)
            def _(i):
                s = page_scores(p, i, q, within, a, b, zero)
                m_ref[...] = jnp.maximum(m_ref[...], jnp.max(s, axis=0, keepdims=True))

        raise_max(res, RES // NP, rma, rmb)
        raise_max(pool, INC // NP, lma, lmb)
        m = m_ref[...]
        start_sums(new_ref, own_scores(new_ref, q), m, l_ref, acc_ref)
        pages_sum(res, RES // NP, 1, q, within, rma, rmb, m, l_ref, acc_ref)
        pages_sum(pool, INC // NP, 1, q, within, lma, lmb, m, l_ref, acc_ref)

    o = (acc_ref[...] / l_ref[...]).T
    for h in range(H):
        o_ref[:, h * HD : (h + 1) * HD] = o[h * PAGE : (h + 1) * PAGE, :].astype(jnp.bfloat16)


def row_shape(n):
    return jax.ShapeDtypeStruct((n, R), jnp.float32)


def resident_call(tab, dec_q, dec_new, resident):
    return pl.pallas_call(
        resident_kernel,
        out_shape=[row_shape(1), row_shape(1), row_shape(HD)],
        in_specs=[VMEM_ALL] * 4,
        out_specs=[VMEM_ALL] * 3,
        scratch_shapes=[
            pltpu.VMEM((RES, R), jnp.float32),
            pltpu.VMEM((RES, R), jnp.float32),
            pltpu.VMEM((R, HD), jnp.bfloat16),
        ],
        compiler_params=pltpu.CompilerParams(vmem_limit_bytes=12 * MIB),
        cost_estimate=pl.CostEstimate(
            flops=4 * R * 8192 * HD * 8, bytes_accessed=5 * MIB, transcendentals=R * 8192
        ),
        name="decode_resident",
    )(tab, dec_q, dec_new, resident)


def handed_call(ids, info, tab, dec_q, dec_new, resident, sums, blocks):
    n = len(blocks)
    return pl.pallas_call(
        functools.partial(handed_kernel, n),
        out_shape=jax.ShapeDtypeStruct((PAGE, H * HD), jnp.bfloat16),
        in_specs=[SMEM_ALL] * 2 + [VMEM_ALL] * 3 + [HBM_ALL] + [VMEM_ALL] * 3 + [HBM_ALL] * n,
        out_specs=VMEM_ALL,
        scratch_shapes=[
            pltpu.VMEM((INC, PAGE, 2 * HD), jnp.bfloat16),
            pltpu.VMEM((R, HD), jnp.bfloat16),
            pltpu.VMEM((INC, R), jnp.float32),
            pltpu.VMEM((INC, R), jnp.float32),
            pltpu.VMEM((RES, R), jnp.float32),
            pltpu.VMEM((RES, R), jnp.float32),
            pltpu.VMEM((RES, PAGE, 2 * HD), jnp.bfloat16),
            pltpu.VMEM((1, R), jnp.float32),
            pltpu.VMEM((1, R), jnp.float32),
            pltpu.VMEM((HD, R), jnp.float32),
            pltpu.SemaphoreType.DMA((INC,)),
            pltpu.SMEM((1,), jnp.int32),
        ],
        compiler_params=pltpu.CompilerParams(vmem_limit_bytes=12 * MIB),
        cost_estimate=pl.CostEstimate(
            flops=4 * R * 1024 * HD * 8, bytes_accessed=2 * MIB, transcendentals=R * 1024
        ),
        name="decode_handed",
    )(ids, info, tab, dec_q, dec_new, in_hbm(resident), *sums, *[in_hbm(b) for b in blocks])


def project_kernel(nblocks, info, w_ref, *refs):
    a_refs = refs[:nblocks]
    o_ref, rows = refs[nblocks:]
    me = info[0]
    for s in range(2 * nblocks):
        r, i = source(s)
        j = ((me - s // 4 * 4) ^ (s % 4)) & 15
        rows[pl.ds(pl.multiple_of(j * PAGE, PAGE), PAGE), :] = a_refs[r][i]
    o_ref[...] = jnp.dot(rows[...], w_ref[...], preferred_element_type=jnp.float32).astype(jnp.bfloat16)


def project_call(info, w, blocks):
    vmem = pl.BlockSpec(memory_space=pltpu.VMEM)
    return pl.pallas_call(
        functools.partial(project_kernel, len(blocks)),
        out_shape=jax.ShapeDtypeStruct((512, w.shape[1]), jnp.bfloat16),
        in_specs=[pl.BlockSpec(memory_space=pltpu.SMEM), vmem] + [vmem] * len(blocks),
        out_specs=vmem,
        scratch_shapes=[pltpu.VMEM((512, w.shape[0]), jnp.bfloat16)],
        compiler_params=pltpu.CompilerParams(vmem_limit_bytes=6 * MIB),
        cost_estimate=pl.CostEstimate(
            flops=2 * 512 * w.shape[0] * w.shape[1], bytes_accessed=3 * MIB, transcendentals=0
        ),
        name="project",
    )(info, w, *blocks)


def swap(x, bit):
    return lax.ppermute(x, "ctx", [(i, i ^ bit) for i in range(16)])


def turn(x, s):
    return lax.ppermute(x, "ctx", [(i, (i + 4 * s) % 16) for i in range(16)])


def after(x, y):
    return lax.optimization_barrier((x, y))[0]


def gather_ctx(x, z_gate):
    x = x[None]
    pair = jnp.concatenate([x, after(swap(x, 2), z_gate)], axis=0)
    across = {s: turn(pair, s) for s in (1, 3, 2)}
    across[0] = pair
    near = {0: swap(pair, 1)}

    def finish(y_gate):
        for s in (1, 3, 2):
            across[s] = after(across[s], y_gate)
            near[s] = swap(across[s], 1)
        return [a[s] for s in range(4) for a in (across, near)]

    return finish


def shards(
    prompt_lens, pre_q, pre_kv, owners, resident, page_table, cache_len, dec_q, dec_new, out_weight
):
    me = lax.axis_index("ctx").astype(jnp.int32)
    info = jnp.concatenate([me[None], prompt_lens.astype(jnp.int32)])

    owned = owners == me
    at = jnp.arange(256, dtype=jnp.int32)
    rank = jnp.sum((owned[None, :] & (at[None, :] < at[:, None])).astype(jnp.int32), axis=1)
    hit = owned[None, :] & (rank[None, :] == jnp.arange(INC, dtype=jnp.int32)[:, None])
    ids = jnp.sum(jnp.where(hit, at[None, :], 0), axis=1)
    ids = jnp.concatenate([ids, jnp.sum(owned.astype(jnp.int32))[None]])

    slot = jnp.where(page_table < 4096, page_table - me * RES, page_table - 4096 + RES)
    col = jnp.arange(PAGE, dtype=jnp.int32)
    end = (cache_len - 1) // PAGE
    last = jnp.sum(jnp.where(col[None, :] == end[:, None], slot, 0), axis=1)
    rem = cache_len - end * PAGE
    slot = jnp.where(col[None, :] <= end[:, None], slot, -1)
    tab = jnp.concatenate([slot.T, last[None], rem[None], jnp.zeros((6, PAGE), jnp.int32)], axis=0)
    tab = jnp.tile(tab, (1, H))

    own = pre_kv[None]
    pair = jnp.concatenate([own, swap(own, 2)], axis=0)
    near = swap(pair, 1)
    up, down = turn(pair, 1), turn(pair, 3)
    sums = resident_call(after(tab, pair), dec_q, dec_new, resident)
    up, down, _ = lax.optimization_barrier((up, down, sums[1]))
    up_near = swap(up, 1)
    far = turn(after(pair, up), 2)
    m, *state = prefill_call("first", 0, FIRST, info, pre_q, [pair, near, up, up_near])
    far, down = after(far, state[0]), after(down, state[0])
    blocks = [pair, near, up, up_near, far, swap(far, 1), down, swap(down, 1)]
    dec = handed_call(ids, info, tab, dec_q, dec_new, resident, sums, blocks)
    state = prefill_call("middle", FIRST, FIRST + 2, after(info, dec), pre_q, blocks, (m, *state))
    finish = gather_ctx(dec, state[0])
    state = prefill_call("middle", FIRST + 2, FIRST + 4, info, pre_q, blocks, (m, *state))
    part = project_call(info, out_weight, finish(state[0]))
    attended = prefill_call("final", FIRST + 4, 16, after(info, part), pre_q, blocks, (m, *state))
    part = lax.all_to_all(part.reshape(8, 64, 512), "grp", split_axis=0, concat_axis=0, tiled=True)
    decoded = jnp.sum(part.astype(jnp.float32), axis=0).astype(jnp.bfloat16)
    return attended, decoded


def solution(mesh):
    return jax.shard_map(
        shards,
        mesh=mesh,
        in_specs=(
            P(),
            P("ctx", "grp"),
            P("ctx", "grp"),
            P(),
            P("ctx", None, "grp"),
            P("ctx", None),
            P("ctx"),
            P("ctx", "grp"),
            P("ctx", "grp"),
            P("grp", "ctx"),
        ),
        out_specs=(P("ctx", "grp"), P("grp", "ctx")),
        check_vma=False,
    )
```

```python
import functools
import math

import jax
import jax.numpy as jnp
from jax import lax
from jax.experimental import pallas as pl
from jax.experimental.pallas import tpu as pltpu
from jax.sharding import PartitionSpec as P

HD = 128
T = 512
H = 8
PAGE = 32
NEG = -1e30
BIG = 2.0**100
C = HD**-0.5 * math.log2(math.e)
RES = 256
INC = 32
FIRST = 4
MIB = 2**20


SMEM_ALL = pl.BlockSpec(memory_space=pltpu.SMEM)
VMEM_ALL = pl.BlockSpec(memory_space=pltpu.VMEM)
HBM_ALL = pl.BlockSpec(memory_space=pltpu.HBM)


def in_hbm(x):
    return pltpu.with_memory_space_constraint(x, pltpu.HBM)


def dot_t(a, b):
    return lax.dot_general(a, b, (((1,), (1,)), ((), ())), preferred_element_type=jnp.float32)


def segment_starts(ends, t):
    start = jnp.zeros_like(t)
    for e in ends:
        start = jnp.maximum(start, jnp.where(t >= e, e, 0))
    return start


def source(s):
    return s // 4 * 2 + s % 2, s % 4 // 2


def prefill_kernel(kind, nblocks, first, last, info, *refs):
    nref = 1 + nblocks
    q_ref, kv_refs = refs[0], refs[1:nref]
    count = 2 * nblocks
    if kind == "first":
        m_ref, l_ref, acc_ref, buf, vx, start, row, bias, sem, use = refs[nref:]
    elif kind == "middle":
        m_ref, l_in, acc_in, l_ref, acc_ref, buf, vx, start, row, bias, sem, use = refs[nref:]
    else:
        m_in, l_in, acc_in, o_ref, m_ref, l_ref, acc_ref, q_buf = refs[nref : nref + 8]
        l_add, acc_add, buf, vx, start, row, bias, sem, use, sem_in, fail = refs[nref + 8 :]
        moves = [
            pltpu.make_async_copy(a, b, sem_in.at[i])
            for i, (a, b) in enumerate(((q_ref, q_buf), (m_in, m_ref), (l_in, l_add), (acc_in, acc_add)))
        ]
        for c in moves:
            c.start()
        q_ref = q_buf
    me = info[0]
    t0 = me * T
    e0 = info[1]
    e1 = e0 + info[2]
    e2 = e1 + info[3]
    ends = (e0, e1, e2)
    lo = segment_starts(ends, t0)

    def block_of(s):
        c = s // 4
        return (me - 4 * c) ^ (s - 4 * c)

    def needed(s):
        j = block_of(s)
        return (j >= 0) & (j <= me) & (lo < (j + 1) * T)

    def choose(a, b):
        number = jnp.int32(0)
        for s in range(count):
            n = needed(s)
            use[s] = jnp.where(n & (number >= a) & (number < b), 1, 0)
            number += n.astype(jnp.int32)

    def fetch():
        for s in range(count):
            @pl.when(use[s] == 1)
            def _():
                r, k = source(s)
                pltpu.make_async_copy(kv_refs[r].at[k], buf.at[s], sem.at[s]).start()

    def await_slot(s):
        pltpu.make_async_copy(kv_refs[0].at[0], buf.at[s], sem.at[s]).wait()

    def set_bias(j):
        u = j * T + lax.broadcasted_iota(jnp.int32, (T, T), 1)
        t = t0 + lax.broadcasted_iota(jnp.int32, (T, 1), 0)
        ok = (u <= t) & (u >= start[:, :1])
        bias[...] = jnp.where(ok, 0.0, NEG)

    def scores(h, k, masked):
        s = dot_t(q_ref[:, pl.ds(pl.multiple_of(h * HD, HD), HD)], k) * C
        return s + bias[...] if masked else s

    def max_block(s):
        set_bias(block_of(s))
        k = buf[s, :, :HD]

        @pl.loop(0, H)
        def _(h):
            x = jnp.max(scores(h, k, True), axis=1, keepdims=True)
            m_ref[h] = jnp.maximum(m_ref[h], jnp.broadcast_to(x, (T, HD)))

    def add_block(s, masked, fresh=False):
        k = buf[s, :, :HD]
        vx[:, :HD] = buf[s, :, HD:]
        v = vx[...]

        def rest(h, x):
            if fresh:
                m = jnp.broadcast_to(jnp.max(x, axis=1, keepdims=True), (T, HD))
                m_ref[h] = m
            else:
                m = m_ref[h] if masked else m_ref[h] + row[...]
            p = jnp.exp2(x - jnp.concatenate([m] * (T // HD), axis=1))
            pv = jnp.dot(p.astype(jnp.bfloat16), v, preferred_element_type=jnp.float32)
            if fresh:
                l_ref[h] = pv[:, HD:]
                acc_ref[h] = pv[:, :HD]
            else:
                l_ref[h] += pv[:, HD:]
                acc_ref[h] += pv[:, :HD]

        @pl.loop(0, H // 4)
        def _(g):
            x = scores(g * 4, k, masked)
            for i in range(4):
                y = scores(g * 4 + i + 1, k, masked) if i < 3 else None
                rest(g * 4 + i, x)
                x = y

    def sweep(a, b, wait):
        @pl.loop(a, b)
        def _(s):
            @pl.when(use[s] == 1)
            def _():
                if wait:
                    await_slot(s)
                j = block_of(s)
                masked = j == me
                for e in ends:
                    masked |= (e > j * T) & (e < (j + 1) * T)

                @pl.when(masked)
                def _():
                    set_bias(j)
                    add_block(s, True)

                @pl.when(jnp.logical_not(masked))
                def _():
                    row[...] = jnp.where(start[...] >= (j + 1) * T, -NEG, 0.0)
                    add_block(s, False)

    def clear():
        l_ref[...] = jnp.zeros_like(l_ref)
        acc_ref[...] = jnp.zeros_like(acc_ref)

    choose(first, last)
    fetch()
    start[...] = segment_starts(ends, t0 + lax.broadcasted_iota(jnp.int32, (T, HD), 0))
    vx[:, HD:] = jnp.ones((T, HD), jnp.bfloat16)
    if kind == "first":
        await_slot(0)
        set_bias(me)
        add_block(0, True, fresh=True)
        sweep(1, count, True)
        return
    if kind == "final":
        clear()
        for c in moves[:2]:
            c.wait()
    else:
        l_ref[...] = l_in[...]
        acc_ref[...] = acc_in[...]
    sweep(0, count, True)
    if kind == "final":
        for c in moves[2:]:
            c.wait()
        fail[0] = jnp.where(jnp.max(jnp.where(l_ref[...] + l_add[...] < BIG, 0.0, 1.0)) > 0.0, 1, 0)

        @pl.when(fail[0] == 1)
        def _():
            l_add[...] = jnp.zeros_like(l_add)
            acc_add[...] = jnp.zeros_like(acc_add)
            choose(0, first)
            fetch()

            @pl.loop(0, count)
            def _(s):
                @pl.when(use[s] == 1)
                def _():
                    await_slot(s)

            clear()
            choose(0, count)

            @pl.loop(0, count)
            def _(s):
                @pl.when(use[s] == 1)
                def _():
                    max_block(s)

            sweep(0, count, False)

        for h in range(H):
            o_ref[:, h * HD : (h + 1) * HD] = (
                (acc_ref[h] + acc_add[h]) / (l_ref[h] + l_add[h])
            ).astype(jnp.bfloat16)


def prefill_call(kind, first, last, info, q, blocks, state=()):
    count = 2 * len(blocks)
    carry = jax.ShapeDtypeStruct((H, T, HD), jnp.float32)
    vmem = pl.BlockSpec(memory_space=pltpu.VMEM)
    scratch = [
        pltpu.VMEM((count, T, 2 * HD), jnp.bfloat16),
        pltpu.VMEM((T, 2 * HD), jnp.bfloat16),
        pltpu.VMEM((T, HD), jnp.int32),
        pltpu.VMEM((T, HD), jnp.float32),
        pltpu.VMEM((T, T), jnp.float32),
        pltpu.SemaphoreType.DMA((count,)),
        pltpu.SMEM((count,), jnp.int32),
    ]
    if kind == "final":
        scratch = (
            [pltpu.VMEM((H, T, HD), jnp.float32)] * 3
            + [pltpu.VMEM((T, H * HD), jnp.bfloat16)]
            + [pltpu.VMEM((H, T, HD), jnp.float32)] * 2
            + scratch
            + [pltpu.SemaphoreType.DMA((4,)), pltpu.SMEM((1,), jnp.int32)]
        )
        out_shape, out_specs = jax.ShapeDtypeStruct((T, H * HD), jnp.bfloat16), vmem
    else:
        n = 3 if kind == "first" else 2
        out_shape, out_specs = [carry] * n, [vmem] * n
    work = last - first
    blocks = [in_hbm(b) for b in blocks]
    data = vmem
    if kind == "final":
        q, state, data = in_hbm(q), [in_hbm(x) for x in state], HBM_ALL
    return pl.pallas_call(
        functools.partial(prefill_kernel, kind, len(blocks), first, last),
        out_shape=out_shape,
        in_specs=[SMEM_ALL, data] + [HBM_ALL] * len(blocks) + [data] * len(state),
        out_specs=out_specs,
        scratch_shapes=scratch,
        compiler_params=pltpu.CompilerParams(vmem_limit_bytes=(27 if kind == "final" else 14) * MIB),
        cost_estimate=pl.CostEstimate(
            flops=work * H * T * T * HD * 8, bytes_accessed=8 * MIB, transcendentals=work * H * T * T
        ),
        name="prefill_" + kind,
    )(info, q, *blocks, *state)


R = H * PAGE
NP = 16


def page_counts(tab_ref, lma, lmb, first, groups):
    last = tab_ref[PAGE : PAGE + 1, :]

    @pl.loop(0, groups)
    def _(g):
        page = first + g * 32 + lax.broadcasted_iota(jnp.int32, (32, R), 0)
        n = jnp.zeros((32, R), jnp.float32)
        for j in range(32):
            n += jnp.where(tab_ref[j : j + 1, :] == page, 1.0, 0.0)
        fewer = n - jnp.where(page == last, 1.0, 0.0)
        at = pl.ds(pl.multiple_of(g * 32, 32), 32)
        lma[at, :] = jnp.where(n > 0.5, jnp.log2(jnp.maximum(n, 1.0)), NEG)
        lmb[at, :] = jnp.where(fewer > 0.5, jnp.log2(jnp.maximum(fewer, 1.0)), NEG)


def load_queries(q_ref, qs):
    for h in range(H):
        qs[h * PAGE : (h + 1) * PAGE, :] = q_ref[:, h * HD : (h + 1) * HD]


def page_scores(pool, b, q, within, lma, lmb, m):
    k = pool[pl.ds(b * NP, NP), :, :HD].reshape(NP * PAGE, HD)
    s = (dot_t(k, q) * C).reshape(NP, PAGE, R)
    at = pl.ds(pl.multiple_of(b * NP, NP), NP)
    a = (lma[at, :] - m)[:, None, :]
    return (s + jnp.where(within[None], a, (lmb[at, :] - m)[:, None, :])).reshape(NP * PAGE, R)


def pages_sum(pool, blocks, per, q, within, lma, lmb, m, l_ref, acc_ref):
    @pl.loop(0, blocks // per)
    def _(g):
        l = l_ref[...]
        acc = acc_ref[...]
        x = page_scores(pool, g * per, q, within, lma, lmb, m)
        for i in range(per):
            b = g * per + i
            y = page_scores(pool, b + 1, q, within, lma, lmb, m) if i < per - 1 else None
            v = pool[pl.ds(b * NP, NP), :, HD:].reshape(NP * PAGE, HD)
            p = jnp.exp2(x)
            l = l + jnp.sum(p, axis=0, keepdims=True)
            acc = acc + lax.dot_general(
                v, p.astype(jnp.bfloat16), (((0,), (0,)), ((), ())),
                preferred_element_type=jnp.float32,
            )
            x = y
        l_ref[...] = l
        acc_ref[...] = acc


def own_scores(new_ref, q):
    own = dot_t(new_ref[:, :HD], q) * C
    row = lax.broadcasted_iota(jnp.int32, (PAGE, R), 0)
    mine = row == (lax.broadcasted_iota(jnp.int32, (PAGE, R), 1) & (PAGE - 1))
    return jnp.where(mine, own, NEG)


def start_sums(new_ref, own, m, l_ref, acc_ref):
    p = jnp.exp2(own - m)
    l_ref[...] = jnp.sum(p, axis=0, keepdims=True)
    acc_ref[...] = lax.dot_general(
        new_ref[:, HD:], p.astype(jnp.bfloat16), (((0,), (0,)), ((), ())),
        preferred_element_type=jnp.float32,
    )


def rows_within(tab_ref):
    return lax.broadcasted_iota(jnp.int32, (PAGE, R), 0) < tab_ref[PAGE + 1 : PAGE + 2, :]


def resident_kernel(tab_ref, q_ref, new_ref, pool, m_ref, l_ref, acc_ref, lma, lmb, qs):
    load_queries(q_ref, qs)
    q = qs[...]
    own = own_scores(new_ref, q)
    m = jnp.max(own, axis=0, keepdims=True)
    m_ref[...] = m
    page_counts(tab_ref, lma, lmb, 0, RES // 32)
    start_sums(new_ref, own, m, l_ref, acc_ref)
    pages_sum(pool, RES // NP, 4, q, rows_within(tab_ref), lma, lmb, m, l_ref, acc_ref)


def handed_kernel(nblocks, ids, info, tab_ref, q_ref, new_ref, res_ref, m_in, l_in, acc_in, *refs):
    kv_refs = refs[:nblocks]
    o_ref, pool, qs, lma, lmb, rma, rmb, res, m_ref, l_ref, acc_ref, sem, fail = refs[nblocks:]
    me = info[0]
    pool[...] = jnp.zeros((INC, PAGE, 2 * HD), jnp.bfloat16)
    n_owned = ids[INC]

    @pl.loop(0, n_owned)
    def _(k):
        page = ids[k]
        j = page // 16
        c = (me // 4 - j // 4) & 3
        b = (me ^ j) & 3
        at = pl.ds(pl.multiple_of((page % 16) * PAGE, PAGE), PAGE)
        r = 2 * c + (b & 1)
        for i in range(nblocks):
            @pl.when(r == i)
            def _():
                pltpu.make_async_copy(kv_refs[i].at[b // 2, at], pool.at[k], sem.at[k]).start()

    load_queries(q_ref, qs)
    q = qs[...]
    within = rows_within(tab_ref)
    page_counts(tab_ref, lma, lmb, RES, INC // 32)
    m_ref[...] = m_in[...]
    l_ref[...] = l_in[...]
    acc_ref[...] = acc_in[...]

    @pl.loop(0, n_owned)
    def _(k):
        pltpu.make_async_copy(kv_refs[0].at[0, pl.ds(0, PAGE)], pool.at[k], sem.at[k]).wait()

    pages_sum(pool, INC // NP, 2, q, within, lma, lmb, m_in[...], l_ref, acc_ref)
    fail[0] = jnp.where(jnp.max(jnp.where(l_ref[...] < BIG, 0.0, 1.0)) > 0.0, 1, 0)

    @pl.when(fail[0] == 1)
    def _():
        copy = pltpu.make_async_copy(res_ref, res, sem.at[0])
        copy.start()
        page_counts(tab_ref, rma, rmb, 0, RES // 32)
        copy.wait()
        zero = jnp.zeros((1, R), jnp.float32)

        def raise_max(p, n, a, b):
            @pl.loop(0, n)
            def _(i):
                s = page_scores(p, i, q, within, a, b, zero)
                m_ref[...] = jnp.maximum(m_ref[...], jnp.max(s, axis=0, keepdims=True))

        raise_max(res, RES // NP, rma, rmb)
        raise_max(pool, INC // NP, lma, lmb)
        m = m_ref[...]
        start_sums(new_ref, own_scores(new_ref, q), m, l_ref, acc_ref)
        pages_sum(res, RES // NP, 1, q, within, rma, rmb, m, l_ref, acc_ref)
        pages_sum(pool, INC // NP, 1, q, within, lma, lmb, m, l_ref, acc_ref)

    o = (acc_ref[...] / l_ref[...]).T
    for h in range(H):
        o_ref[:, h * HD : (h + 1) * HD] = o[h * PAGE : (h + 1) * PAGE, :].astype(jnp.bfloat16)


def row_shape(n):
    return jax.ShapeDtypeStruct((n, R), jnp.float32)


def resident_call(tab, dec_q, dec_new, resident):
    return pl.pallas_call(
        resident_kernel,
        out_shape=[row_shape(1), row_shape(1), row_shape(HD)],
        in_specs=[VMEM_ALL] * 4,
        out_specs=[VMEM_ALL] * 3,
        scratch_shapes=[
            pltpu.VMEM((RES, R), jnp.float32),
            pltpu.VMEM((RES, R), jnp.float32),
            pltpu.VMEM((R, HD), jnp.bfloat16),
        ],
        compiler_params=pltpu.CompilerParams(vmem_limit_bytes=12 * MIB),
        cost_estimate=pl.CostEstimate(
            flops=4 * R * 8192 * HD * 8, bytes_accessed=5 * MIB, transcendentals=R * 8192
        ),
        name="decode_resident",
    )(tab, dec_q, dec_new, resident)


def handed_call(ids, info, tab, dec_q, dec_new, resident, sums, blocks):
    n = len(blocks)
    return pl.pallas_call(
        functools.partial(handed_kernel, n),
        out_shape=jax.ShapeDtypeStruct((PAGE, H * HD), jnp.bfloat16),
        in_specs=[SMEM_ALL] * 2 + [VMEM_ALL] * 3 + [HBM_ALL] + [VMEM_ALL] * 3 + [HBM_ALL] * n,
        out_specs=VMEM_ALL,
        scratch_shapes=[
            pltpu.VMEM((INC, PAGE, 2 * HD), jnp.bfloat16),
            pltpu.VMEM((R, HD), jnp.bfloat16),
            pltpu.VMEM((INC, R), jnp.float32),
            pltpu.VMEM((INC, R), jnp.float32),
            pltpu.VMEM((RES, R), jnp.float32),
            pltpu.VMEM((RES, R), jnp.float32),
            pltpu.VMEM((RES, PAGE, 2 * HD), jnp.bfloat16),
            pltpu.VMEM((1, R), jnp.float32),
            pltpu.VMEM((1, R), jnp.float32),
            pltpu.VMEM((HD, R), jnp.float32),
            pltpu.SemaphoreType.DMA((INC,)),
            pltpu.SMEM((1,), jnp.int32),
        ],
        compiler_params=pltpu.CompilerParams(vmem_limit_bytes=12 * MIB),
        cost_estimate=pl.CostEstimate(
            flops=4 * R * 1024 * HD * 8, bytes_accessed=2 * MIB, transcendentals=R * 1024
        ),
        name="decode_handed",
    )(ids, info, tab, dec_q, dec_new, in_hbm(resident), *sums, *[in_hbm(b) for b in blocks])


def project_kernel(nblocks, info, w_ref, *refs):
    a_refs = refs[:nblocks]
    o_ref, rows = refs[nblocks:]
    me = info[0]
    for s in range(2 * nblocks):
        r, i = source(s)
        j = ((me - s // 4 * 4) ^ (s % 4)) & 15
        rows[pl.ds(pl.multiple_of(j * PAGE, PAGE), PAGE), :] = a_refs[r][i]
    o_ref[...] = jnp.dot(rows[...], w_ref[...], preferred_element_type=jnp.float32).astype(jnp.bfloat16)


def project_call(info, w, blocks):
    vmem = pl.BlockSpec(memory_space=pltpu.VMEM)
    return pl.pallas_call(
        functools.partial(project_kernel, len(blocks)),
        out_shape=jax.ShapeDtypeStruct((512, w.shape[1]), jnp.bfloat16),
        in_specs=[pl.BlockSpec(memory_space=pltpu.SMEM), vmem] + [vmem] * len(blocks),
        out_specs=vmem,
        scratch_shapes=[pltpu.VMEM((512, w.shape[0]), jnp.bfloat16)],
        compiler_params=pltpu.CompilerParams(vmem_limit_bytes=6 * MIB),
        cost_estimate=pl.CostEstimate(
            flops=2 * 512 * w.shape[0] * w.shape[1], bytes_accessed=3 * MIB, transcendentals=0
        ),
        name="project",
    )(info, w, *blocks)


def swap(x, bit):
    return lax.ppermute(x, "ctx", [(i, i ^ bit) for i in range(16)])


def turn(x, s):
    return lax.ppermute(x, "ctx", [(i, (i + 4 * s) % 16) for i in range(16)])


def after(x, y):
    return lax.optimization_barrier((x, y))[0]


def gather_ctx(x, z_gate):
    x = x[None]
    pair = jnp.concatenate([x, after(swap(x, 2), z_gate)], axis=0)
    across = {s: turn(pair, s) for s in (1, 3, 2)}
    across[0] = pair
    near = {0: swap(pair, 1)}

    def finish(y_gate):
        for s in (1, 3, 2):
            across[s] = after(across[s], y_gate)
            near[s] = swap(across[s], 1)
        return [a[s] for s in range(4) for a in (across, near)]

    return finish


def shards(
    prompt_lens, pre_q, pre_kv, owners, resident, page_table, cache_len, dec_q, dec_new, out_weight
):
    me = lax.axis_index("ctx").astype(jnp.int32)
    info = jnp.concatenate([me[None], prompt_lens.astype(jnp.int32)])

    owned = owners == me
    at = jnp.arange(256, dtype=jnp.int32)
    rank = jnp.sum((owned[None, :] & (at[None, :] < at[:, None])).astype(jnp.int32), axis=1)
    hit = owned[None, :] & (rank[None, :] == jnp.arange(INC, dtype=jnp.int32)[:, None])
    ids = jnp.sum(jnp.where(hit, at[None, :], 0), axis=1)
    ids = jnp.concatenate([ids, jnp.sum(owned.astype(jnp.int32))[None]])

    slot = jnp.where(page_table < 4096, page_table - me * RES, page_table - 4096 + RES)
    col = jnp.arange(PAGE, dtype=jnp.int32)
    end = (cache_len - 1) // PAGE
    last = jnp.sum(jnp.where(col[None, :] == end[:, None], slot, 0), axis=1)
    rem = cache_len - end * PAGE
    slot = jnp.where(col[None, :] <= end[:, None], slot, -1)
    tab = jnp.concatenate([slot.T, last[None], rem[None], jnp.zeros((6, PAGE), jnp.int32)], axis=0)
    tab = jnp.tile(tab, (1, H))

    own = pre_kv[None]
    pair = jnp.concatenate([own, swap(own, 2)], axis=0)
    near = swap(pair, 1)
    up, down = turn(pair, 1), turn(pair, 3)
    sums = resident_call(after(tab, pair), dec_q, dec_new, resident)
    up, down, _ = lax.optimization_barrier((up, down, sums[1]))
    up_near = swap(up, 1)
    far = turn(after(pair, up), 2)
    m, *state = prefill_call("first", 0, FIRST, info, pre_q, [pair, near, up, up_near])
    far, down = after(far, state[0]), after(down, state[0])
    blocks = [pair, near, up, up_near, far, swap(far, 1), down, swap(down, 1)]
    dec = handed_call(ids, info, tab, dec_q, dec_new, resident, sums, blocks)
    state = prefill_call("middle", FIRST, FIRST + 2, after(info, dec), pre_q, blocks, (m, *state))
    finish = gather_ctx(dec, state[0])
    state = prefill_call("middle", FIRST + 2, FIRST + 4, info, pre_q, blocks, (m, *state))
    part = project_call(info, out_weight, finish(state[0]))
    attended = prefill_call("final", FIRST + 4, 16, after(info, part), pre_q, blocks, (m, *state))
    part = lax.all_to_all(part.reshape(8, 64, 512), "grp", split_axis=0, concat_axis=0, tiled=True)
    decoded = jnp.sum(part.astype(jnp.float32), axis=0).astype(jnp.bfloat16)
    return attended, decoded


def solution(mesh):
    return jax.shard_map(
        shards,
        mesh=mesh,
        in_specs=(
            P(),
            P("ctx", "grp"),
            P("ctx", "grp"),
            P(),
            P("ctx", None, "grp"),
            P("ctx", None),
            P("ctx"),
            P("ctx", "grp"),
            P("ctx", "grp"),
            P("grp", "ctx"),
        ),
        out_specs=(P("ctx", "grp"), P("grp", "ctx")),
        check_vma=False,
    )
```

```python
import functools
import math

import jax
import jax.numpy as jnp
from jax import lax
from jax.experimental import pallas as pl
from jax.experimental.pallas import tpu as pltpu
from jax.sharding import PartitionSpec as P

HD = 128
T = 512
H = 8
PAGE = 32
NEG = -1e30
BIG = 2.0**100
C = HD**-0.5 * math.log2(math.e)
RES = 256
INC = 32
FIRST = 4
MIB = 2**20


SMEM_ALL = pl.BlockSpec(memory_space=pltpu.SMEM)
VMEM_ALL = pl.BlockSpec(memory_space=pltpu.VMEM)
HBM_ALL = pl.BlockSpec(memory_space=pltpu.HBM)


def in_hbm(x):
    return pltpu.with_memory_space_constraint(x, pltpu.HBM)


def head_columns(h):
    return pl.ds(h * HD if isinstance(h, int) else pl.multiple_of(h * HD, HD), HD)


def dot_t(a, b):
    return lax.dot_general(a, b, (((1,), (1,)), ((), ())), preferred_element_type=jnp.float32)


def segment_starts(ends, t):
    start = jnp.zeros_like(t)
    for e in ends:
        start = jnp.maximum(start, jnp.where(t >= e, e, 0))
    return start


def source(s):
    return s // 4 * 2 + s % 2, s % 4 // 2


def prefill_kernel(kind, nblocks, first, last, info, *refs):
    nref = 1 + nblocks
    q_ref, kv_refs = refs[0], refs[1:nref]
    count = 2 * nblocks
    if kind == "first":
        m_ref, l_ref, acc_ref, buf, vx, start, row, bias, sem, use = refs[nref:]
    elif kind == "middle":
        m_ref, l_in, acc_in, l_ref, acc_ref, buf, vx, start, row, bias, sem, use = refs[nref:]
    else:
        m_in, l_in, acc_in, o_ref, m_ref, l_ref, acc_ref, q_buf = refs[nref : nref + 8]
        l_add, acc_add, buf, vx, start, row, bias, sem, use, sem_in, fail = refs[nref + 8 :]
        moves = [
            pltpu.make_async_copy(a, b, sem_in.at[i])
            for i, (a, b) in enumerate(((q_ref, q_buf), (m_in, m_ref), (l_in, l_add), (acc_in, acc_add)))
        ]
        for c in moves:
            c.start()
        q_ref = q_buf
    me = info[0]
    t0 = me * T
    e0 = info[1]
    e1 = e0 + info[2]
    e2 = e1 + info[3]
    ends = (e0, e1, e2)
    lo = segment_starts(ends, t0)

    def block_of(s):
        c = s // 4
        return (me - 4 * c) ^ (s - 4 * c)

    def needed(s):
        j = block_of(s)
        return (j >= 0) & (j <= me) & (lo < (j + 1) * T)

    def choose(a, b):
        number = jnp.int32(0)
        for s in range(count):
            n = needed(s)
            use[s] = jnp.where(n & (number >= a) & (number < b), 1, 0)
            number += n.astype(jnp.int32)

    def fetch():
        for s in range(count):
            @pl.when(use[s] == 1)
            def _():
                r, k = source(s)
                pltpu.make_async_copy(kv_refs[r].at[k], buf.at[s], sem.at[s]).start()

    def await_slot(s):
        pltpu.make_async_copy(kv_refs[0].at[0], buf.at[s], sem.at[s]).wait()

    def set_bias(j):
        u = j * T + lax.broadcasted_iota(jnp.int32, (T, T), 1)
        t = t0 + lax.broadcasted_iota(jnp.int32, (T, 1), 0)
        ok = (u <= t) & (u >= start[:, :1])
        bias[...] = jnp.where(ok, 0.0, NEG)

    def scores(h, k, masked):
        s = dot_t(q_ref[:, head_columns(h)], k) * C
        return s + bias[...] if masked else s

    def max_block(s):
        set_bias(block_of(s))
        k = buf[s, :, :HD]

        @pl.loop(0, H)
        def _(h):
            x = jnp.max(scores(h, k, True), axis=1, keepdims=True)
            m_ref[h] = jnp.maximum(m_ref[h], jnp.broadcast_to(x, (T, HD)))

    def add_block(s, masked, fresh=False):
        k = buf[s, :, :HD]
        vx[:, :HD] = buf[s, :, HD:]
        v = vx[...]

        def rest(h, x):
            if fresh:
                m = jnp.broadcast_to(jnp.max(x, axis=1, keepdims=True), (T, HD))
                m_ref[h] = m
            else:
                m = m_ref[h] if masked else m_ref[h] + row[...]
            p = jnp.exp2(x - jnp.concatenate([m] * (T // HD), axis=1))
            pv = jnp.dot(p.astype(jnp.bfloat16), v, preferred_element_type=jnp.float32)
            if fresh:
                l_ref[h] = pv[:, HD:]
                acc_ref[h] = pv[:, :HD]
            else:
                l_ref[h] += pv[:, HD:]
                acc_ref[h] += pv[:, :HD]

        x = scores(0, k, masked)
        for h in range(H):
            y = scores(h + 1, k, masked) if h < H - 1 else None
            rest(h, x)
            x = y

    def sweep(a, b, wait):
        @pl.loop(a, b)
        def _(s):
            @pl.when(use[s] == 1)
            def _():
                if wait:
                    await_slot(s)
                j = block_of(s)
                masked = j == me
                for e in ends:
                    masked |= (e > j * T) & (e < (j + 1) * T)

                @pl.when(masked)
                def _():
                    set_bias(j)
                    add_block(s, True)

                @pl.when(jnp.logical_not(masked))
                def _():
                    row[...] = jnp.where(start[...] >= (j + 1) * T, -NEG, 0.0)
                    add_block(s, False)

    def clear():
        l_ref[...] = jnp.zeros_like(l_ref)
        acc_ref[...] = jnp.zeros_like(acc_ref)

    choose(first, last)
    fetch()
    start[...] = segment_starts(ends, t0 + lax.broadcasted_iota(jnp.int32, (T, HD), 0))
    vx[:, HD:] = jnp.ones((T, HD), jnp.bfloat16)
    if kind == "first":
        await_slot(0)
        set_bias(me)
        add_block(0, True, fresh=True)
        sweep(1, count, True)
        return
    if kind == "final":
        clear()
        for c in moves[:2]:
            c.wait()
    else:
        l_ref[...] = l_in[...]
        acc_ref[...] = acc_in[...]
    sweep(0, count, True)
    if kind == "final":
        for c in moves[2:]:
            c.wait()
        fail[0] = jnp.where(jnp.max(jnp.where(l_ref[...] + l_add[...] < BIG, 0.0, 1.0)) > 0.0, 1, 0)

        @pl.when(fail[0] == 1)
        def _():
            l_add[...] = jnp.zeros_like(l_add)
            acc_add[...] = jnp.zeros_like(acc_add)
            choose(0, first)
            fetch()

            @pl.loop(0, count)
            def _(s):
                @pl.when(use[s] == 1)
                def _():
                    await_slot(s)

            clear()
            choose(0, count)

            @pl.loop(0, count)
            def _(s):
                @pl.when(use[s] == 1)
                def _():
                    max_block(s)

            sweep(0, count, False)

        for h in range(H):
            o_ref[:, h * HD : (h + 1) * HD] = (
                (acc_ref[h] + acc_add[h]) / (l_ref[h] + l_add[h])
            ).astype(jnp.bfloat16)


def prefill_call(kind, first, last, info, q, blocks, state=()):
    count = 2 * len(blocks)
    carry = jax.ShapeDtypeStruct((H, T, HD), jnp.float32)
    vmem = pl.BlockSpec(memory_space=pltpu.VMEM)
    scratch = [
        pltpu.VMEM((count, T, 2 * HD), jnp.bfloat16),
        pltpu.VMEM((T, 2 * HD), jnp.bfloat16),
        pltpu.VMEM((T, HD), jnp.int32),
        pltpu.VMEM((T, HD), jnp.float32),
        pltpu.VMEM((T, T), jnp.float32),
        pltpu.SemaphoreType.DMA((count,)),
        pltpu.SMEM((count,), jnp.int32),
    ]
    if kind == "final":
        scratch = (
            [pltpu.VMEM((H, T, HD), jnp.float32)] * 3
            + [pltpu.VMEM((T, H * HD), jnp.bfloat16)]
            + [pltpu.VMEM((H, T, HD), jnp.float32)] * 2
            + scratch
            + [pltpu.SemaphoreType.DMA((4,)), pltpu.SMEM((1,), jnp.int32)]
        )
        out_shape, out_specs = jax.ShapeDtypeStruct((T, H * HD), jnp.bfloat16), vmem
    else:
        n = 3 if kind == "first" else 2
        out_shape, out_specs = [carry] * n, [vmem] * n
    work = last - first
    blocks = [in_hbm(b) for b in blocks]
    data = vmem
    if kind == "final":
        q, state, data = in_hbm(q), [in_hbm(x) for x in state], HBM_ALL
    return pl.pallas_call(
        functools.partial(prefill_kernel, kind, len(blocks), first, last),
        out_shape=out_shape,
        in_specs=[SMEM_ALL, data] + [HBM_ALL] * len(blocks) + [data] * len(state),
        out_specs=out_specs,
        scratch_shapes=scratch,
        compiler_params=pltpu.CompilerParams(vmem_limit_bytes=(27 if kind == "final" else 14) * MIB),
        cost_estimate=pl.CostEstimate(
            flops=work * H * T * T * HD * 8, bytes_accessed=8 * MIB, transcendentals=work * H * T * T
        ),
        name="prefill_" + kind,
    )(info, q, *blocks, *state)


R = H * PAGE
NP = 16


def page_counts(tab_ref, lma, lmb, first, groups):
    last = tab_ref[PAGE : PAGE + 1, :]

    @pl.loop(0, groups)
    def _(g):
        page = first + g * 32 + lax.broadcasted_iota(jnp.int32, (32, R), 0)
        n = jnp.zeros((32, R), jnp.float32)
        for j in range(32):
            n += jnp.where(tab_ref[j : j + 1, :] == page, 1.0, 0.0)
        fewer = n - jnp.where(page == last, 1.0, 0.0)
        at = pl.ds(pl.multiple_of(g * 32, 32), 32)
        lma[at, :] = jnp.where(n > 0.5, jnp.log2(jnp.maximum(n, 1.0)), NEG)
        lmb[at, :] = jnp.where(fewer > 0.5, jnp.log2(jnp.maximum(fewer, 1.0)), NEG)


def load_queries(q_ref, qs):
    for h in range(H):
        qs[h * PAGE : (h + 1) * PAGE, :] = q_ref[:, h * HD : (h + 1) * HD]


def page_scores(pool, b, q, within, lma, lmb, m):
    k = pool[pl.ds(b * NP, NP), :, :HD].reshape(NP * PAGE, HD)
    s = (dot_t(k, q) * C).reshape(NP, PAGE, R)
    at = pl.ds(pl.multiple_of(b * NP, NP), NP)
    a = (lma[at, :] - m)[:, None, :]
    return (s + jnp.where(within[None], a, (lmb[at, :] - m)[:, None, :])).reshape(NP * PAGE, R)


def pages_sum(pool, blocks, per, q, within, lma, lmb, m, l_ref, acc_ref):
    @pl.loop(0, blocks // per)
    def _(g):
        l = l_ref[...]
        acc = acc_ref[...]
        x = page_scores(pool, g * per, q, within, lma, lmb, m)
        for i in range(per):
            b = g * per + i
            y = page_scores(pool, b + 1, q, within, lma, lmb, m) if i < per - 1 else None
            v = pool[pl.ds(b * NP, NP), :, HD:].reshape(NP * PAGE, HD)
            p = jnp.exp2(x)
            l = l + jnp.sum(p, axis=0, keepdims=True)
            acc = acc + lax.dot_general(
                v, p.astype(jnp.bfloat16), (((0,), (0,)), ((), ())),
                preferred_element_type=jnp.float32,
            )
            x = y
        l_ref[...] = l
        acc_ref[...] = acc


def own_scores(new_ref, q):
    own = dot_t(new_ref[:, :HD], q) * C
    row = lax.broadcasted_iota(jnp.int32, (PAGE, R), 0)
    mine = row == (lax.broadcasted_iota(jnp.int32, (PAGE, R), 1) & (PAGE - 1))
    return jnp.where(mine, own, NEG)


def start_sums(new_ref, own, m, l_ref, acc_ref):
    p = jnp.exp2(own - m)
    l_ref[...] = jnp.sum(p, axis=0, keepdims=True)
    acc_ref[...] = lax.dot_general(
        new_ref[:, HD:], p.astype(jnp.bfloat16), (((0,), (0,)), ((), ())),
        preferred_element_type=jnp.float32,
    )


def rows_within(tab_ref):
    return lax.broadcasted_iota(jnp.int32, (PAGE, R), 0) < tab_ref[PAGE + 1 : PAGE + 2, :]


def resident_kernel(tab_ref, q_ref, new_ref, pool, m_ref, l_ref, acc_ref, lma, lmb, qs):
    load_queries(q_ref, qs)
    q = qs[...]
    own = own_scores(new_ref, q)
    m = jnp.max(own, axis=0, keepdims=True)
    m_ref[...] = m
    page_counts(tab_ref, lma, lmb, 0, RES // 32)
    start_sums(new_ref, own, m, l_ref, acc_ref)
    pages_sum(pool, RES // NP, 4, q, rows_within(tab_ref), lma, lmb, m, l_ref, acc_ref)


def handed_kernel(nblocks, ids, info, tab_ref, q_ref, new_ref, res_ref, m_in, l_in, acc_in, *refs):
    kv_refs = refs[:nblocks]
    o_ref, pool, qs, lma, lmb, rma, rmb, res, m_ref, l_ref, acc_ref, sem, fail = refs[nblocks:]
    me = info[0]
    pool[...] = jnp.zeros((INC, PAGE, 2 * HD), jnp.bfloat16)
    n_owned = ids[INC]

    @pl.loop(0, n_owned)
    def _(k):
        page = ids[k]
        j = page // 16
        c = (me // 4 - j // 4) & 3
        b = (me ^ j) & 3
        at = pl.ds(pl.multiple_of((page % 16) * PAGE, PAGE), PAGE)
        r = 2 * c + (b & 1)
        for i in range(nblocks):
            @pl.when(r == i)
            def _():
                pltpu.make_async_copy(kv_refs[i].at[b // 2, at], pool.at[k], sem.at[k]).start()

    load_queries(q_ref, qs)
    q = qs[...]
    within = rows_within(tab_ref)
    page_counts(tab_ref, lma, lmb, RES, INC // 32)
    m_ref[...] = m_in[...]
    l_ref[...] = l_in[...]
    acc_ref[...] = acc_in[...]

    @pl.loop(0, n_owned)
    def _(k):
        pltpu.make_async_copy(kv_refs[0].at[0, pl.ds(0, PAGE)], pool.at[k], sem.at[k]).wait()

    pages_sum(pool, INC // NP, 2, q, within, lma, lmb, m_in[...], l_ref, acc_ref)
    fail[0] = jnp.where(jnp.max(jnp.where(l_ref[...] < BIG, 0.0, 1.0)) > 0.0, 1, 0)

    @pl.when(fail[0] == 1)
    def _():
        copy = pltpu.make_async_copy(res_ref, res, sem.at[0])
        copy.start()
        page_counts(tab_ref, rma, rmb, 0, RES // 32)
        copy.wait()
        zero = jnp.zeros((1, R), jnp.float32)

        def raise_max(p, n, a, b):
            @pl.loop(0, n)
            def _(i):
                s = page_scores(p, i, q, within, a, b, zero)
                m_ref[...] = jnp.maximum(m_ref[...], jnp.max(s, axis=0, keepdims=True))

        raise_max(res, RES // NP, rma, rmb)
        raise_max(pool, INC // NP, lma, lmb)
        m = m_ref[...]
        start_sums(new_ref, own_scores(new_ref, q), m, l_ref, acc_ref)
        pages_sum(res, RES // NP, 1, q, within, rma, rmb, m, l_ref, acc_ref)
        pages_sum(pool, INC // NP, 1, q, within, lma, lmb, m, l_ref, acc_ref)

    o = (acc_ref[...] / l_ref[...]).T
    for h in range(H):
        o_ref[:, h * HD : (h + 1) * HD] = o[h * PAGE : (h + 1) * PAGE, :].astype(jnp.bfloat16)


def row_shape(n):
    return jax.ShapeDtypeStruct((n, R), jnp.float32)


def resident_call(tab, dec_q, dec_new, resident):
    return pl.pallas_call(
        resident_kernel,
        out_shape=[row_shape(1), row_shape(1), row_shape(HD)],
        in_specs=[VMEM_ALL] * 4,
        out_specs=[VMEM_ALL] * 3,
        scratch_shapes=[
            pltpu.VMEM((RES, R), jnp.float32),
            pltpu.VMEM((RES, R), jnp.float32),
            pltpu.VMEM((R, HD), jnp.bfloat16),
        ],
        compiler_params=pltpu.CompilerParams(vmem_limit_bytes=12 * MIB),
        cost_estimate=pl.CostEstimate(
            flops=4 * R * 8192 * HD * 8, bytes_accessed=5 * MIB, transcendentals=R * 8192
        ),
        name="decode_resident",
    )(tab, dec_q, dec_new, resident)


def handed_call(ids, info, tab, dec_q, dec_new, resident, sums, blocks):
    n = len(blocks)
    return pl.pallas_call(
        functools.partial(handed_kernel, n),
        out_shape=jax.ShapeDtypeStruct((PAGE, H * HD), jnp.bfloat16),
        in_specs=[SMEM_ALL] * 2 + [VMEM_ALL] * 3 + [HBM_ALL] + [VMEM_ALL] * 3 + [HBM_ALL] * n,
        out_specs=VMEM_ALL,
        scratch_shapes=[
            pltpu.VMEM((INC, PAGE, 2 * HD), jnp.bfloat16),
            pltpu.VMEM((R, HD), jnp.bfloat16),
            pltpu.VMEM((INC, R), jnp.float32),
            pltpu.VMEM((INC, R), jnp.float32),
            pltpu.VMEM((RES, R), jnp.float32),
            pltpu.VMEM((RES, R), jnp.float32),
            pltpu.VMEM((RES, PAGE, 2 * HD), jnp.bfloat16),
            pltpu.VMEM((1, R), jnp.float32),
            pltpu.VMEM((1, R), jnp.float32),
            pltpu.VMEM((HD, R), jnp.float32),
            pltpu.SemaphoreType.DMA((INC,)),
            pltpu.SMEM((1,), jnp.int32),
        ],
        compiler_params=pltpu.CompilerParams(vmem_limit_bytes=12 * MIB),
        cost_estimate=pl.CostEstimate(
            flops=4 * R * 1024 * HD * 8, bytes_accessed=2 * MIB, transcendentals=R * 1024
        ),
        name="decode_handed",
    )(ids, info, tab, dec_q, dec_new, in_hbm(resident), *sums, *[in_hbm(b) for b in blocks])


def project_kernel(nblocks, info, w_ref, *refs):
    a_refs = refs[:nblocks]
    o_ref, rows = refs[nblocks:]
    me = info[0]
    for s in range(2 * nblocks):
        r, i = source(s)
        j = ((me - s // 4 * 4) ^ (s % 4)) & 15
        rows[pl.ds(pl.multiple_of(j * PAGE, PAGE), PAGE), :] = a_refs[r][i]
    o_ref[...] = jnp.dot(rows[...], w_ref[...], preferred_element_type=jnp.float32).astype(jnp.bfloat16)


def project_call(info, w, blocks):
    vmem = pl.BlockSpec(memory_space=pltpu.VMEM)
    return pl.pallas_call(
        functools.partial(project_kernel, len(blocks)),
        out_shape=jax.ShapeDtypeStruct((512, w.shape[1]), jnp.bfloat16),
        in_specs=[pl.BlockSpec(memory_space=pltpu.SMEM), vmem] + [vmem] * len(blocks),
        out_specs=vmem,
        scratch_shapes=[pltpu.VMEM((512, w.shape[0]), jnp.bfloat16)],
        compiler_params=pltpu.CompilerParams(vmem_limit_bytes=6 * MIB),
        cost_estimate=pl.CostEstimate(
            flops=2 * 512 * w.shape[0] * w.shape[1], bytes_accessed=3 * MIB, transcendentals=0
        ),
        name="project",
    )(info, w, *blocks)


def swap(x, bit):
    return lax.ppermute(x, "ctx", [(i, i ^ bit) for i in range(16)])


def turn(x, s):
    return lax.ppermute(x, "ctx", [(i, (i + 4 * s) % 16) for i in range(16)])


def after(x, y):
    return lax.optimization_barrier((x, y))[0]


def gather_ctx(x, z_gate):
    x = x[None]
    pair = jnp.concatenate([x, after(swap(x, 2), z_gate)], axis=0)
    across = {s: turn(pair, s) for s in (1, 3, 2)}
    across[0] = pair
    near = {0: swap(pair, 1)}

    def finish(y_gate):
        for s in (1, 3, 2):
            across[s] = after(across[s], y_gate)
            near[s] = swap(across[s], 1)
        return [a[s] for s in range(4) for a in (across, near)]

    return finish


def shards(
    prompt_lens, pre_q, pre_kv, owners, resident, page_table, cache_len, dec_q, dec_new, out_weight
):
    me = lax.axis_index("ctx").astype(jnp.int32)
    info = jnp.concatenate([me[None], prompt_lens.astype(jnp.int32)])

    owned = owners == me
    at = jnp.arange(256, dtype=jnp.int32)
    rank = jnp.sum((owned[None, :] & (at[None, :] < at[:, None])).astype(jnp.int32), axis=1)
    hit = owned[None, :] & (rank[None, :] == jnp.arange(INC, dtype=jnp.int32)[:, None])
    ids = jnp.sum(jnp.where(hit, at[None, :], 0), axis=1)
    ids = jnp.concatenate([ids, jnp.sum(owned.astype(jnp.int32))[None]])

    slot = jnp.where(page_table < 4096, page_table - me * RES, page_table - 4096 + RES)
    col = jnp.arange(PAGE, dtype=jnp.int32)
    end = (cache_len - 1) // PAGE
    last = jnp.sum(jnp.where(col[None, :] == end[:, None], slot, 0), axis=1)
    rem = cache_len - end * PAGE
    slot = jnp.where(col[None, :] <= end[:, None], slot, -1)
    tab = jnp.concatenate([slot.T, last[None], rem[None], jnp.zeros((6, PAGE), jnp.int32)], axis=0)
    tab = jnp.tile(tab, (1, H))

    own = pre_kv[None]
    pair = jnp.concatenate([own, swap(own, 2)], axis=0)
    near = swap(pair, 1)
    up, down = turn(pair, 1), turn(pair, 3)
    sums = resident_call(after(tab, pair), dec_q, dec_new, resident)
    up, down, _ = lax.optimization_barrier((up, down, sums[1]))
    up_near = swap(up, 1)
    far = turn(after(pair, up), 2)
    m, *state = prefill_call("first", 0, FIRST, info, pre_q, [pair, near, up, up_near])
    far, down = after(far, state[0]), after(down, state[0])
    blocks = [pair, near, up, up_near, far, swap(far, 1), down, swap(down, 1)]
    dec = handed_call(ids, info, tab, dec_q, dec_new, resident, sums, blocks)
    state = prefill_call("middle", FIRST, FIRST + 2, after(info, dec), pre_q, blocks, (m, *state))
    finish = gather_ctx(dec, state[0])
    state = prefill_call("middle", FIRST + 2, FIRST + 4, info, pre_q, blocks, (m, *state))
    part = project_call(info, out_weight, finish(state[0]))
    attended = prefill_call("final", FIRST + 4, 16, after(info, part), pre_q, blocks, (m, *state))
    part = lax.all_to_all(part.reshape(8, 64, 512), "grp", split_axis=0, concat_axis=0, tiled=True)
    decoded = jnp.sum(part.astype(jnp.float32), axis=0).astype(jnp.bfloat16)
    return attended, decoded


def solution(mesh):
    return jax.shard_map(
        shards,
        mesh=mesh,
        in_specs=(
            P(),
            P("ctx", "grp"),
            P("ctx", "grp"),
            P(),
            P("ctx", None, "grp"),
            P("ctx", None),
            P("ctx"),
            P("ctx", "grp"),
            P("ctx", "grp"),
            P("grp", "ctx"),
        ),
        out_specs=(P("ctx", "grp"), P("grp", "ctx")),
        check_vma=False,
    )
```
